256 devices in a mesh: gx: 8 (over z), gy: 4 (over y), gz: 8 (over x, core).
Axes of the slice: x: 4, y: 4, z: 8, core: 2. Of those that a mesh axis runs over, the one named last changes fastest.
Arguments:
- subspace: bfloat16 [64, 192, 256, 128], P('gx', 'gy', 'gz'), may hold values from -45 to 45, as said below
- potential: float32 [64, 192, 256], P('gx', 'gy', 'gz'), may hold values from -3 to 1
Outputs:
- density: float32 [64, 192, 256], P('gx', 'gy', 'gz')
- energy_density: float32 [64, 192, 256], P('gx', 'gy', 'gz')
The draws below stay inside these ranges and needn't reach their ends.
Inputs may be any that keep to these rules, and one draw needn't show every extreme that they name: `subspace`: vectors 0 to 63 are the current orbitals, vectors 64 to 127 the preconditioned residuals.
All inputs are finite; a program needn't handle non-finite values.
Results may differ from the reference program's by a relative error of at most 0.0045.
Values may be sent and summed in bfloat16 or wider, within the bound.
A program may use at most 64 MiB of HBM per device.

```python
import math
import jax
import jax.numpy as jnp
from jax import lax

NB = 64
NS = 128
CX = 8
FILTER_STEPS = 8
NX = 64
NY = 192
NZ = 256


def grid_axis(count):
    return 2.0 * jnp.arange(count, dtype=jnp.float32) / count - 1.0


def smooth_fields(key):
    key_wave, key_phase = jax.random.split(key)
    waves = jax.random.randint(key_wave, (8, 3), 1, 4).astype(jnp.float32)
    phases = jax.random.uniform(key_phase, (8, 3), jnp.float32, -math.pi, math.pi)
    tables = []
    for column, count in enumerate((NX, NY, NZ)):
        turns = 2.0 * math.pi * jnp.arange(count, dtype=jnp.float32) / count
        tables.append(math.sqrt(2.0) * jnp.cos(waves[:, column, None] * turns[None, :] + phases[:, column, None]))
    return tables


def draw_subspace(key, part):
    key = jax.random.fold_in(key, 11)
    key_basis, key_mix, key_slope, key_noise = jax.random.split(key, 4)
    along_x, along_y, along_z = smooth_fields(key_basis)
    smooth_amp = jnp.concatenate([jnp.ones((NB,), jnp.float32), jnp.full((NB,), 0.5, jnp.float32)])
    noise_amp = jnp.concatenate([jnp.full((NB,), 0.7, jnp.float32), jnp.ones((NB,), jnp.float32)])
    weights = jax.random.normal(key_mix, (8, NS), jnp.float32) / math.sqrt(8.0)
    noise = jax.random.normal(key_noise, (NX, NY, NZ, NS), jnp.float32) * noise_amp
    weights = weights * smooth_amp[None, :]
    smooth = jnp.zeros((NX, NY, NZ, NS), jnp.float32)
    for index in range(8):
        field = along_x[index][:, None, None, None] * along_y[index][None, :, None, None] * along_z[index][None, None, :, None]
        smooth = smooth + field * weights[index][None, None, None, :]
    slopes = jax.random.uniform(key_slope, (3, NS), jnp.float32, -0.8, 0.8)
    exponent = slopes[0][None, None, None, :] * grid_axis(NX)[:, None, None, None]
    exponent = exponent + slopes[1][None, None, None, :] * grid_axis(NY)[None, :, None, None]
    exponent = exponent + slopes[2][None, None, None, :] * grid_axis(NZ)[None, None, :, None]
    return (jnp.clip(smooth + noise, -4.0, 4.0) * jnp.exp(exponent)).astype(jnp.bfloat16)


def level_of(key, dims, shards, smallest, top_value):
    loudness, own = 1.0, jax.random.fold_in(key, 6)
    for axis_at, blocks in shards:
        steps = jnp.exp(jax.random.uniform(jax.random.fold_in(own, axis_at), (blocks,), jnp.float32, smallest / len(shards), top_value / len(shards)))
        loudness = loudness * jnp.repeat(steps, dims[axis_at] // blocks).reshape([-1 if axis == axis_at else 1 for axis in range(len(dims))])
    return loudness


def setup_inputs(seed: int = 0) -> dict:
    key_list = jax.random.split(jax.random.key(seed), 3)
    subspace = draw_subspace(jax.random.fold_in(key_list[2], 71), 0)
    potential = jnp.clip(-3.0 + 4.0 * jax.random.uniform(key_list[1], (NX, NY, NZ), jnp.float32) ** level_of(key_list[1], (NX, NY, NZ), ((0, 8), (1, 4), (2, 8)), -0.2, 0.2), -3.0, 1.0)
    return dict(subspace=subspace, potential=potential)


stencil = (-1.0 / 12.0, 4.0 / 3.0, -2.5, 4.0 / 3.0, -1.0 / 12.0)

def second_diff(values, axis_id):
    count = values.shape[axis_id] - 4
    total = stencil[0] * lax.slice_in_dim(values, 0, count, axis=axis_id).astype(jnp.float32)
    for offset in range(1, 5):
        total = total + stencil[offset] * lax.slice_in_dim(values, offset, offset + count, axis=axis_id).astype(jnp.float32)
    return total

def make_projector(correlation, hamil):
    identity = jnp.eye(correlation.shape[0], dtype=jnp.float32)
    symmetric = 0.5 * (hamil + hamil.T)
    factor = jnp.linalg.cholesky(correlation)
    left_solve = lax.linalg.triangular_solve(factor, symmetric, left_side=True, lower=True)
    reduced = lax.linalg.triangular_solve(factor, left_solve.T, left_side=True, lower=True)
    reduced = 0.5 * (reduced + reduced.T)
    shifted = reduced - jnp.trace(reduced) / reduced.shape[0] * identity
    sign_matrix = shifted / jnp.sqrt(jnp.sum(shifted * shifted) + 1e-06)
    for repeat in range(FILTER_STEPS):
        square = jnp.dot(sign_matrix, sign_matrix, precision=lax.Precision.HIGHEST)
        sign_matrix = 1.5 * sign_matrix - 0.5 * jnp.dot(square, sign_matrix, precision=lax.Precision.HIGHEST)
    projector = 0.5 * (identity - sign_matrix)
    half_solve = lax.linalg.triangular_solve(factor, projector, left_side=True, lower=True, transpose_a=True)
    rotation = lax.linalg.triangular_solve(factor, half_solve.T, left_side=True, lower=True, transpose_a=True)
    return (0.5 * (rotation + rotation.T)).astype(jnp.bfloat16)

def take_slab(subspace, start):
    rows_index = start - 2 + jnp.arange(CX + 4, dtype=jnp.int32)
    valid = ((rows_index >= 0) & (rows_index < NX)).astype(subspace.dtype)
    rows = jnp.take(subspace, jnp.clip(rows_index, 0, NX - 1).astype(jnp.int32), axis=0)
    return rows * valid[:, None, None, None]

def slab_terms(subspace, potential, start):
    widened = take_slab(subspace, start)
    padded = jnp.pad(widened, ((0, 0), (2, 2), (2, 2), (0, 0)))
    laplace = second_diff(padded[:, 2:-2, 2:-2], 0) + second_diff(padded[2:-2, :, 2:-2], 1) + second_diff(padded[2:-2, 2:-2, :], 2)
    center = widened[2:-2]
    pot_slab = lax.dynamic_slice_in_dim(potential, start, CX, 0)
    applied = (-0.5 * laplace + pot_slab[..., None] * center.astype(jnp.float32)).astype(jnp.bfloat16)
    return (center.reshape(-1, NS), applied.reshape(-1, NS))

def reference(subspace, potential):
    count = NX // CX
    ncell = float(NX * NY * NZ)
    contract = (((0,), (0,)), ((), ()))

    def accumulate(sums, slab_id):
        center, applied = slab_terms(subspace, potential, slab_id * CX)
        over_part = sums[0] + lax.dot_general(center.astype(jnp.float32), center.astype(jnp.float32), contract, preferred_element_type=jnp.float32)
        hamil_part = sums[1] + lax.dot_general(center.astype(jnp.float32), applied.astype(jnp.float32), contract, preferred_element_type=jnp.float32)
        return ((over_part, hamil_part), None)
    zeros = jnp.zeros((NS, NS), jnp.float32)
    (correlation, hamil), unused = lax.scan(accumulate, (zeros, zeros), jnp.arange(count, dtype=jnp.int32))
    rotation = make_projector(correlation / ncell, hamil / ncell)

    def outputs(slab_id):
        center, applied = slab_terms(subspace, potential, slab_id * CX)
        mixed = jnp.dot(center.astype(jnp.float32), rotation.astype(jnp.float32), preferred_element_type=jnp.float32)
        charge = lax.optimization_barrier(jnp.sum(center.astype(jnp.float32) * mixed, axis=1)) / NB
        energy = lax.optimization_barrier(jnp.sum(applied.astype(jnp.float32) * mixed, axis=1)) / NB
        return (charge.reshape(CX, NY, NZ), energy.reshape(CX, NY, NZ))
    charge, energy = lax.map(outputs, jnp.arange(count, dtype=jnp.int32))
    return (charge.reshape(NX, NY, NZ), energy.reshape(NX, NY, NZ))
```

```python
import jax
import jax.numpy as jnp
from jax import lax
from jax.experimental import pallas as pl
from jax.experimental.pallas import tpu as pltpu
from jax.sharding import PartitionSpec as P

NB = 64
FILTER_STEPS = 8
MESH = pl.DeviceIdType.MESH


stencil = (-1.0 / 12.0, 4.0 / 3.0, -2.5, 4.0 / 3.0, -1.0 / 12.0)


def with_halo(block, sides, width):
    for axis, dim in sides:
        count = lax.axis_size(axis)
        forward = [(i, i + 1) for i in range(count - 1)]
        backward = [(target, source) for source, target in forward]
        low = lax.ppermute(
            lax.slice_in_dim(block, block.shape[dim] - width, None, axis=dim), axis, forward
        )
        high = lax.ppermute(lax.slice_in_dim(block, 0, width, axis=dim), axis, backward)
        block = jnp.concatenate([low, block, high], axis=dim)
    return block


def second_diff(values, axis_id):
    count = values.shape[axis_id] - 4
    total = stencil[0] * lax.slice_in_dim(values, 0, count, axis=axis_id).astype(jnp.float32)
    for offset in range(1, 5):
        total = total + stencil[offset] * lax.slice_in_dim(
            values, offset, offset + count, axis=axis_id
        ).astype(jnp.float32)
    return total


AXES = ("gx", "gy", "gz")


def place(axis, index):
    return tuple(index if name == axis else lax.axis_index(name) for name in AXES)


def all_reduce_kernel(sizes, x_ref, o_ref, part, got_z, got_x, got_y, send_sem, recv_sem):
    rows = part.shape[0]
    nx, ny, nz = sizes
    me = {name: lax.axis_index(name) for name in AXES}
    size = dict(zip(AXES, sizes))

    barrier = pltpu.get_barrier_semaphore()
    for axis in AXES:
        for off in range(1, size[axis]):
            peer = lax.rem(me[axis] + off, size[axis])
            pl.semaphore_signal(barrier, inc=1, device_id=place(axis, peer), device_id_type=MESH)
    pl.semaphore_wait(barrier, nx + ny + nz - 3)

    def exchange(stage, axis, source, target):
        copies = []
        for off in range(1, size[axis]):
            peer = lax.rem(me[axis] + off, size[axis])
            copy = pltpu.make_async_remote_copy(
                src_ref=source(peer),
                dst_ref=target,
                send_sem=send_sem.at[stage],
                recv_sem=recv_sem.at[stage],
                device_id=place(axis, peer),
                device_id_type=MESH,
            )
            copy.start()
            copies.append(copy)
        return copies

    def finish(stage, count, like):
        whole = like.at[pl.ds(0, count)]
        pltpu.make_async_copy(whole, whole, recv_sem.at[stage]).wait()
        pltpu.make_async_copy(whole, whole, send_sem.at[stage]).wait()

    exchange(0, "gz", lambda peer: x_ref.at[peer], got_z.at[me["gz"]])
    got_z[me["gz"]] = x_ref[me["gz"]]
    finish(0, nz - 1, got_z)
    part[...] = sum(got_z[i] for i in range(1, nz)) + got_z[0]

    exchange(1, "gy", lambda peer: part, got_y.at[me["gy"]])
    got_y[me["gy"]] = part[...]
    finish(1, ny - 1, got_y)
    part2 = sum(got_y[i] for i in range(1, ny)) + got_y[0]
    got_x[me["gx"]] = part2

    exchange(2, "gx", lambda peer: got_x.at[me["gx"]], got_x.at[me["gx"]])
    finish(2, nx - 1, got_x)
    o_ref[me["gz"]] = sum(got_x[i] for i in range(1, nx)) + got_x[0]

    exchange(3, "gz", lambda peer: o_ref.at[me["gz"]], o_ref.at[me["gz"]])
    finish(3, nz - 1, o_ref)


def all_reduce(value):
    sizes = tuple(lax.axis_size(name) for name in AXES)
    nx, ny, nz = sizes
    rows = value.shape[0] // nz
    import functools

    out = pl.pallas_call(
        functools.partial(all_reduce_kernel, sizes),
        out_shape=jax.ShapeDtypeStruct((nz, rows, value.shape[1]), jnp.float32),
        in_specs=[pl.BlockSpec(memory_space=pltpu.VMEM)],
        out_specs=pl.BlockSpec(memory_space=pltpu.VMEM),
        scratch_shapes=[
            pltpu.VMEM((rows, value.shape[1]), jnp.float32),
            pltpu.VMEM((nz, rows, value.shape[1]), jnp.float32),
            pltpu.VMEM((nx, rows, value.shape[1]), jnp.float32),
            pltpu.VMEM((ny, rows, value.shape[1]), jnp.float32),
            pltpu.SemaphoreType.DMA((4,)),
            pltpu.SemaphoreType.DMA((4,)),
        ],
        compiler_params=pltpu.CompilerParams(collective_id=0, has_side_effects=True),
    )(value.reshape(nz, rows, value.shape[1]))
    return out.reshape(value.shape)


def make_projector(correlation, hamil):
    identity = jnp.eye(correlation.shape[0], dtype=jnp.float32)
    symmetric = 0.5 * (hamil + hamil.T)
    factor = jnp.linalg.cholesky(correlation)
    left_solve = lax.linalg.triangular_solve(factor, symmetric, left_side=True, lower=True)
    reduced = lax.linalg.triangular_solve(factor, left_solve.T, left_side=True, lower=True)
    reduced = 0.5 * (reduced + reduced.T)
    shifted = reduced - jnp.trace(reduced) / reduced.shape[0] * identity
    sign_matrix = shifted / jnp.sqrt(jnp.sum(shifted * shifted) + 1e-06)
    for repeat in range(FILTER_STEPS):
        square = jnp.dot(sign_matrix, sign_matrix, precision=lax.Precision.HIGHEST)
        sign_matrix = 1.5 * sign_matrix - 0.5 * jnp.dot(
            square, sign_matrix, precision=lax.Precision.HIGHEST
        )
    projector = 0.5 * (identity - sign_matrix)
    half_solve = lax.linalg.triangular_solve(
        factor, projector, left_side=True, lower=True, transpose_a=True
    )
    rotation = lax.linalg.triangular_solve(
        factor, half_solve.T, left_side=True, lower=True, transpose_a=True
    )
    return (0.5 * (rotation + rotation.T)).astype(jnp.bfloat16)


def body(subspace, potential):
    width = subspace.shape[3]
    ncell = float(
        subspace.shape[0]
        * subspace.shape[1]
        * subspace.shape[2]
        * lax.axis_size("gx")
        * lax.axis_size("gy")
        * lax.axis_size("gz")
    )
    contract = (((0,), (0,)), ((), ()))
    flat = subspace.reshape(-1, width)
    extended = with_halo(subspace, (("gx", 0), ("gy", 1), ("gz", 2)), 2)
    laplace = (
        second_diff(extended[:, 2:-2, 2:-2], 0)
        + second_diff(extended[2:-2, :, 2:-2], 1)
        + second_diff(extended[2:-2, 2:-2, :], 2)
    )
    applied = (-0.5 * laplace + potential[..., None] * subspace.astype(jnp.float32)).astype(
        jnp.bfloat16
    )
    applied_flat = applied.reshape(-1, width)
    local_hamil = lax.dot_general(flat, applied_flat, contract, preferred_element_type=jnp.float32)
    local_over = lax.dot_general(flat, flat, contract, preferred_element_type=jnp.float32)
    both = all_reduce(jnp.concatenate([local_over, local_hamil], axis=0))
    correlation, hamil = both[:width], both[width:]
    rotation = make_projector(correlation / ncell, hamil / ncell)
    mixed = jnp.dot(flat, rotation, preferred_element_type=jnp.float32)
    charge = jnp.sum(flat.astype(jnp.float32) * mixed, axis=1) / NB
    energy = jnp.sum(applied_flat.astype(jnp.float32) * mixed, axis=1) / NB
    return (charge.reshape(potential.shape), energy.reshape(potential.shape))


def solution(mesh):
    return jax.shard_map(
        body,
        mesh=mesh,
        in_specs=(P("gx", "gy", "gz", None), P("gx", "gy", "gz")),
        out_specs=(P("gx", "gy", "gz"), P("gx", "gy", "gz")),
        check_vma=False,
    )
```

```python
import functools

import jax
import jax.numpy as jnp
from jax import lax
from jax.experimental import pallas as pl
from jax.experimental.pallas import tpu as pltpu
from jax.sharding import PartitionSpec as P

NB = 64
FILTER_STEPS = 8
MESH = pl.DeviceIdType.MESH
AXES = ("gx", "gy", "gz")
F32, BF16 = jnp.float32, jnp.bfloat16

CX, CY, CZ, NV = 8, 48, 32, 128
CELLS = CX * CZ
HALF = CY // 2
LOADS = 4
PIECES = 4
LATE = 2
ZPIECES = 2


def place(axis, index):
    return tuple(index if name == axis else lax.axis_index(name) for name in AXES)


def iota(shape, dim):
    return lax.broadcasted_iota(jnp.int32, shape, dim)


def tap(distance):
    return jnp.where(distance == 1, 16.0, 0.0) - jnp.where(distance == 2, 1.0, 0.0)


def dot_nn(a, b):
    return jnp.dot(a, b, preferred_element_type=F32)


def dot_nt(a, b):
    return lax.dot_general(a, b, (((1,), (1,)), ((), ())), preferred_element_type=F32)


def exact(a, b):
    return jnp.dot(a, b, precision=lax.Precision.HIGHEST, preferred_element_type=F32)


def exact_nt(a, b):
    return lax.dot_general(
        a, b, (((1,), (1,)), ((), ())), precision=lax.Precision.HIGHEST, preferred_element_type=F32
    )


def kernel(
    sizes, u_hbm, pot_hbm, dens_out, en_out,
    u_v, ut, appl, hx, hy, hz, zs, xc, potv, pott, at, ez, bt, bg, pz, eye,
    c_in, c_z, c_y, c_x, c_out, h_in, h_z, h_y, h_x, h_out, mat, linv, linvt, rows_d, rows_e,
    load_sem, x_send, x_recv, y_send, y_recv, z_send, z_recv, ar_send, ar_recv,
):
    size = dict(zip(AXES, sizes))
    me = {name: lax.axis_index(name) for name in AXES}
    gx, gy, gz = me["gx"], me["gy"], me["gz"]
    nx, ny, nz = sizes
    ncell = float(nx * ny * nz * CX * CY * CZ)

    per = CY // LOADS
    loads = []
    for i in range(LOADS):
        span = pl.ds(i * per, per)
        loads.append(pltpu.make_async_copy(u_hbm.at[:, span], u_v.at[:, span], load_sem.at[i]))
        loads[-1].start()
    pot_load = pltpu.make_async_copy(pot_hbm, potv, load_sem.at[LOADS])
    pot_load.start()

    barrier = pltpu.get_barrier_semaphore()
    for axis in AXES:
        for off in range(1, size[axis]):
            peer = lax.rem(me[axis] + off, size[axis])
            pl.semaphore_signal(barrier, inc=1, device_id=place(axis, peer), device_id_type=MESH)
    pl.semaphore_wait(barrier, nx + ny + nz - 3)

    def send(src, dst, ssem, rsem, axis, peer):
        return pltpu.make_async_remote_copy(
            src_ref=src, dst_ref=dst, send_sem=ssem, recv_sem=rsem,
            device_id=place(axis, peer), device_id_type=MESH,
        )

    def x_copy(side, start, count, slot):
        layers = pl.ds(CX - 2, 2) if side == 0 else pl.ds(0, 2)
        span = pl.ds(start, count)
        peer = lax.rem(gx + 1, nx) if side == 0 else lax.rem(gx + nx - 1, nx)
        return send(
            u_hbm.at[layers, span], hx.at[side, :, span],
            x_send.at[side, slot], x_recv.at[side, slot], "gx", peer,
        )

    early_n, late_n = HALF // PIECES, HALF // LATE

    def x_early(side, i):
        return x_copy(side, (HALF if side == 0 else 0) + i * early_n, early_n, i)

    def x_late(side, i):
        return x_copy(side, (0 if side == 0 else HALF) + i * late_n, late_n, PIECES + i)

    def y_copy(side):
        layers = pl.ds(CY - 2, 2) if side == 0 else pl.ds(0, 2)
        peer = lax.rem(gy + 1, ny) if side == 0 else lax.rem(gy + ny - 1, ny)
        return send(
            u_hbm.at[:, layers], hy.at[side], y_send.at[side], y_recv.at[side], "gy", peer
        )

    def z_copy(side, i):
        span = pl.ds(i * (CY // ZPIECES), CY // ZPIECES)
        peer = lax.rem(gz + 1, nz) if side == 0 else lax.rem(gz + nz - 1, nz)
        return send(
            zs.at[span, side], hz.at[span, side],
            z_send.at[side, i], z_recv.at[side, i], "gz", peer,
        )

    def sends(axis, side):
        return me[axis] < size[axis] - 1 if side == 0 else me[axis] > 0

    def receives(axis, side):
        return me[axis] > 0 if side == 0 else me[axis] < size[axis] - 1

    for side in range(2):
        @pl.when(sends("gy", side))
        def _():
            y_copy(side).start()

    for i in range(PIECES):
        for side in range(2):
            @pl.when(sends("gx", side))
            def _():
                x_early(side, i).start()

    for side in range(2):
        @pl.when(jnp.logical_not(receives("gx", side)))
        def _():
            def clear(y, carry):
                hx[side, :, y] = jnp.zeros((2, CZ, NV), BF16)
                return carry
            lax.fori_loop(0, CY, clear, 0)

        @pl.when(jnp.logical_not(receives("gy", side)))
        def _():
            hy[side] = jnp.zeros((CX, 2, CZ, NV), BF16)

        @pl.when(jnp.logical_not(receives("gz", side)))
        def _():
            def clear(y, carry):
                hz[y, side] = jnp.zeros((2 * CX, NV), BF16)
                return carry
            lax.fori_loop(0, CY, clear, 0)

    eye[...] = jnp.where(iota((NV, NV), 0) == iota((NV, NV), 1), 1.0, 0.0).astype(BF16)

    r, c = iota((CELLS, CELLS), 0), iota((CELLS, CELLS), 1)
    same_x, same_z = (r >> 5) == (c >> 5), (r & 31) == (c & 31)
    along_z = jnp.where(same_x, tap(jnp.abs((r & 31) - (c & 31))), 0.0)
    along_x = jnp.where(same_z, tap(jnp.abs((r >> 5) - (c >> 5))), 0.0)
    at[...] = (along_x + along_z - jnp.where(r == c, 90.0, 0.0)).astype(BF16)

    r, c = iota((NV, CELLS), 0), iota((NV, CELLS), 1)
    k, x = (r >> 5) & 1, c >> 5
    dist = jnp.where(r < 64, x + 2 - k, CX + k - x)
    bt[...] = jnp.where((r & 31) == (c & 31), tap(dist), 0.0).astype(BF16)

    r, c = iota((2 * CELLS, NV), 0), iota((2 * CELLS, NV), 1)
    k, x = (c >> 5) & 1, (r >> 5) & 7
    dist = jnp.where(c < 64, CX + k - x, x + 2 - k)
    keep = ((r & 31) == (c & 31)) & ((r < CELLS) == (c < 64))
    bg[...] = jnp.where(keep, tap(dist), 0.0).astype(BF16)

    for j in range(4):
        r, c = iota((NV, CELLS), 0), iota((NV, CELLS), 1)
        k, z = r & 1, c & 31
        dist = jnp.where(((r >> 4) & 1) == 0, z + 2 - k, CZ + k - z)
        keep = ((r >> 5) == j) & (((r >> 1) & 7) == (c >> 5))
        ez[j] = jnp.where(keep, tap(dist), 0.0).astype(BF16)

    r, c = iota((32, CELLS), 0), iota((32, CELLS), 1)
    target = jnp.where(r < 16, CZ - 2, 0) + (r & 1)
    pz[...] = jnp.where(
        (((r >> 1) & 7) == (c >> 5)) & ((c & 31) == target), 1.0, 0.0
    ).astype(BF16)

    c_in[...] = jnp.zeros_like(c_in)
    h_in[...] = jnp.zeros_like(h_in)

    def add_to(total, value):
        rows = NV // nz
        total[...] += value.reshape(nz, rows, NV)

    def turn(i, carry):
        part = None
        for j in range(4):
            y = i * 4 + j
            block = u_v[:, y].reshape(CELLS, NV)
            turned = dot_nt(eye[...], block).astype(BF16)
            ut[y + 2] = turned
            zs[y] = dot_nn(pz[...], block).astype(BF16).reshape(2, 2 * CX, NV)
            term = dot_nn(turned, block)
            part = term if part is None else part + term
        add_to(c_in, part)
        return carry

    for i in range(LOADS):
        loads[i].wait()
        lax.fori_loop(i * per // 4, (i + 1) * per // 4, turn, 0)
        if (i + 1) % (LOADS // ZPIECES) == 0:
            for side in range(2):
                @pl.when(sends("gz", side))
                def _():
                    z_copy(side, i // (LOADS // ZPIECES)).start()

    def exchange(stage, axis, source, target):
        for off in range(1, size[axis]):
            peer = lax.rem(me[axis] + off, size[axis])
            send(source(peer), target, ar_send.at[stage], ar_recv.at[stage], axis, peer).start()

    def finish(stage, axis, like):
        whole = like.at[pl.ds(0, size[axis] - 1)]
        pltpu.make_async_copy(whole, whole, ar_recv.at[stage]).wait()
        pltpu.make_async_copy(whole, whole, ar_send.at[stage]).wait()

    def total(ref, count):
        out = ref[0]
        for i in range(1, count):
            out = out + ref[i]
        return out

    def stage0(base, source, z):
        exchange(base, "gz", lambda peer: source.at[peer], z.at[gz])
        z[gz] = source[gz]

    def stage1(base, z, y):
        finish(base, "gz", z)
        y[gy] = total(z, nz)
        exchange(base + 1, "gy", lambda peer: y.at[gy], y.at[gy])

    def stage2(base, y, x):
        finish(base + 1, "gy", y)
        x[gx] = total(y, ny)
        exchange(base + 2, "gx", lambda peer: x.at[gx], x.at[gx])

    def stage3(base, x, out):
        finish(base + 2, "gx", x)
        out[gz] = total(x, nx)
        exchange(base + 3, "gz", lambda peer: out.at[gz], out.at[gz])

    stage0(0, c_in, c_z)

    pot_load.wait()
    pott[...] = potv[...].reshape(CELLS, CY).T

    for side in range(2):
        @pl.when(receives("gy", side))
        def _():
            y_copy(side).wait_recv()
        for k in range(2):
            ut[(0 if side == 0 else CY + 2) + k] = dot_nt(
                eye[...], hy[side, :, k].reshape(CELLS, NV)
            ).astype(BF16)

    def apply(i, carry):
        halo = dot_nt(eye[...], hz[pl.ds(i * 4, 4)].reshape(NV, NV)).astype(BF16)
        part = None
        for j in range(4):
            y = i * 4 + j
            own = ut[y + 2]
            acc = dot_nn(own, at[...]) + dot_nn(halo, ez[j])
            near = ut[y + 1].astype(F32) + ut[y + 3].astype(F32)
            far = ut[y].astype(F32) + ut[y + 4].astype(F32)
            acc = acc + (16.0 * near - far)
            value = acc * (-1.0 / 24.0) + pott[pl.ds(y, 1), :] * own.astype(F32)
            appl[y] = value
            term = dot_nt(own, value.astype(BF16))
            part = term if part is None else part + term
        add_to(h_in, part)
        return carry

    groups = CY // ZPIECES // 4
    for i in range(ZPIECES):
        for side in range(2):
            @pl.when(receives("gz", side))
            def _():
                z_copy(side, i).wait_recv()
        lax.fori_loop(i * groups, (i + 1) * groups, apply, 0)
        if i == 0:
            stage1(0, c_z, c_y)
    stage2(0, c_y, c_x)

    def cross(i, carry):
        for j in range(2):
            p = i * 2 + j
            pair = jnp.concatenate([ut[p + 2], ut[p + 2 + HALF]], axis=1)
            xc[p] = (dot_nn(pair, bg[...]) * (-1.0 / 12.0)).astype(BF16)
        return carry

    lax.fori_loop(0, HALF // 2, cross, 0)
    stage3(0, c_x, c_out)

    for i in range(PIECES):
        for side in range(2):
            @pl.when(receives("gx", side))
            def _():
                x_early(side, i).wait_recv()
        part = None
        for j in range(early_n):
            p = i * early_n + j
            layers = jnp.concatenate(
                [hx[1, :, p].reshape(2 * CZ, NV), hx[0, :, p + HALF].reshape(2 * CZ, NV)], axis=0
            )
            term = dot_nn(xc[p], layers)
            part = term if part is None else part + term
        add_to(h_in, part)

    stage0(4, h_in, h_z)
    for i in range(LATE):
        for side in range(2):
            @pl.when(sends("gx", side))
            def _():
                x_late(side, i).start()

    finish(3, "gz", c_out)
    mat[...] = c_out[...].reshape(NV, NV) * (1.0 / ncell)

    def eliminate(b, carry):
        whole = mat[...]
        panel = mat[pl.ds(pl.multiple_of(b * 8, 8), 8), :]
        row_of, lane_of = iota((NV, NV), 0), iota((NV, NV), 1)
        prow, plane = iota((8, NV), 0), iota((8, NV), 1)
        for s in range(8):
            pivot_row = panel[s : s + 1, :]
            scale = 1.0 / panel[s : s + 1, s : s + 1]
            scaled = jnp.where(plane[:1] == s, scale, pivot_row * scale)
            below = row_of > b * 8 + s
            factor = jnp.where(below, jnp.broadcast_to(whole[:, s : s + 1], (NV, NV)), 0.0)
            whole = jnp.where(below & (lane_of == s), 0.0, whole) - factor * scaled
            if s < 7:
                below = prow > s
                factor = jnp.where(below, jnp.broadcast_to(panel[:, s : s + 1], (8, NV)), 0.0)
                panel = jnp.where(below & (plane == s), 0.0, panel) - factor * scaled
        mat[...] = pltpu.roll(whole, NV - 8, 1)
        return carry

    lax.fori_loop(0, 5, eliminate, 0)
    stage1(4, h_z, h_y)
    lax.fori_loop(5, 10, eliminate, 0)
    stage2(4, h_y, h_x)
    lax.fori_loop(10, 16, eliminate, 0)
    stage3(4, h_x, h_out)

    row_of, lane_of = iota((NV, NV), 0), iota((NV, NV), 1)
    one = jnp.where(row_of == lane_of, 1.0, 0.0)
    done = mat[...]
    diag = jnp.sum(done * one, axis=1, keepdims=True)
    lower = jnp.where(row_of > lane_of, done, one * 1.0) * lax.rsqrt(diag)
    lower = jnp.where(row_of >= lane_of, lower, 0.0)
    linv[...] = lower
    linvt[...] = lower.T

    def widen(i, carry):
        for j in range(2):
            y = i * 2 + j
            halo = dot_nt(eye[...], hx[:, :, y].reshape(NV, NV)).astype(BF16)
            appl[y] += dot_nn(halo, bt[...]) * (-1.0 / 24.0)
        return carry

    for i in range(LATE):
        for side in range(2):
            @pl.when(receives("gx", side))
            def _():
                x_late(side, i).wait_recv()
    lax.fori_loop(0, CY // 2, widen, 0)

    finish(7, "gz", h_out)
    lower = linv[...]
    hamil = h_out[...].reshape(NV, NV) * (1.0 / ncell)
    reduced = exact_nt(exact(lower, hamil), lower)
    reduced = 0.5 * (reduced + reduced.T)
    shifted = reduced - one * (jnp.sum(reduced * one) / NV)
    sign = shifted * lax.rsqrt(jnp.full((1, 1), jnp.sum(shifted * shifted) + 1e-06, F32))
    for step in range(FILTER_STEPS):
        square = exact(sign, sign)
        sign = 1.5 * sign - 0.5 * exact(square, sign)
    rot = exact(linvt[...], exact(0.5 * (one - sign), lower))
    rot = (0.5 * (rot + rot.T)).astype(BF16)

    def densities(i, carry):
        for j in range(2):
            y = i * 2 + j
            own = ut[y + 2]
            mixed = dot_nn(rot, own)
            rows_d[pl.ds(y, 1), :] = jnp.sum(own.astype(F32) * mixed, axis=0, keepdims=True)
            rows_e[pl.ds(y, 1), :] = jnp.sum(appl[y] * mixed, axis=0, keepdims=True)
        return carry

    lax.fori_loop(0, CY // 2, densities, 0)
    dens_out[...] = (rows_d[...].T * (1.0 / NB)).reshape(CX, CZ, CY)
    en_out[...] = (rows_e[...].T * (1.0 / NB)).reshape(CX, CZ, CY)

    for side in range(2):
        @pl.when(sends("gx", side))
        def _():
            for i in range(PIECES):
                x_early(side, i).wait_send()
            for i in range(LATE):
                x_late(side, i).wait_send()

        @pl.when(sends("gy", side))
        def _():
            y_copy(side).wait_send()

        @pl.when(sends("gz", side))
        def _():
            for i in range(ZPIECES):
                z_copy(side, i).wait_send()


def body(subspace, potential):
    sizes = tuple(lax.axis_size(name) for name in AXES)
    nx, ny, nz = sizes
    rows = NV // nz
    vm, dma = pltpu.VMEM, pltpu.SemaphoreType.DMA
    any_space = pl.BlockSpec(memory_space=pl.ANY)
    whole = pl.BlockSpec(memory_space=pltpu.VMEM)
    out = jax.ShapeDtypeStruct((CX, CZ, CY), F32)
    reduce_set = [
        vm((nz, rows, NV), F32), vm((nz, rows, NV), F32), vm((ny, rows, NV), F32),
        vm((nx, rows, NV), F32), vm((nz, rows, NV), F32),
    ]
    density, energy = pl.pallas_call(
        functools.partial(kernel, sizes),
        out_shape=(out, out),
        in_specs=[any_space, any_space],
        out_specs=(whole, whole),
        scratch_shapes=[
            vm((CX, CY, CZ, NV), BF16),
            vm((CY + 4, NV, CELLS), BF16),
            vm((CY, NV, CELLS), F32),
            vm((2, 2, CY, CZ, NV), BF16),
            vm((2, CX, 2, CZ, NV), BF16),
            vm((CY, 2, 2 * CX, NV), BF16),
            vm((CY, 2, 2 * CX, NV), BF16),
            vm((HALF, NV, NV), BF16),
            vm((CX, CZ, CY), F32),
            vm((CY, CELLS), F32),
            vm((CELLS, CELLS), BF16),
            vm((4, NV, CELLS), BF16),
            vm((NV, CELLS), BF16),
            vm((2 * CELLS, NV), BF16),
            vm((32, CELLS), BF16),
            vm((NV, NV), BF16),
            *reduce_set,
            *reduce_set,
            vm((NV, NV), F32),
            vm((NV, NV), F32),
            vm((NV, NV), F32),
            vm((CY, CELLS), F32),
            vm((CY, CELLS), F32),
            dma((LOADS + 1,)),
            dma((2, PIECES + LATE)),
            dma((2, PIECES + LATE)),
            dma((2,)),
            dma((2,)),
            dma((2, ZPIECES)),
            dma((2, ZPIECES)),
            dma((8,)),
            dma((8,)),
        ],
        compiler_params=pltpu.CompilerParams(
            collective_id=0, has_side_effects=True, vmem_limit_bytes=48 * 1024 * 1024
        ),
    )(subspace, jnp.transpose(potential, (0, 2, 1)))
    return jnp.transpose(density, (0, 2, 1)), jnp.transpose(energy, (0, 2, 1))


def solution(mesh):
    return jax.shard_map(
        body,
        mesh=mesh,
        in_specs=(P("gx", "gy", "gz", None), P("gx", "gy", "gz")),
        out_specs=(P("gx", "gy", "gz"), P("gx", "gy", "gz")),
        check_vma=False,
    )
```

```python
import functools

import jax
import jax.numpy as jnp
from jax import lax
from jax.experimental import pallas as pl
from jax.experimental.pallas import tpu as pltpu
from jax.sharding import PartitionSpec as P

NB = 64
FILTER_STEPS = 8
MESH = pl.DeviceIdType.MESH
AXES = ("gx", "gy", "gz")
F32, BF16 = jnp.float32, jnp.bfloat16

CX, CY, CZ, NV = 8, 48, 32, 128
CELLS = CX * CZ
HALF = CY // 2
LOADS = 4
PIECES = 4
LATE = 2
ZPIECES = 2
STACK = 8


def place(axis, index):
    return tuple(index if name == axis else lax.axis_index(name) for name in AXES)


def iota(shape, dim):
    return lax.broadcasted_iota(jnp.int32, shape, dim)


def tap(distance):
    return jnp.where(distance == 1, 16.0, 0.0) - jnp.where(distance == 2, 1.0, 0.0)


def dot_nn(a, b):
    return jnp.dot(a, b, preferred_element_type=F32)


def dot_nt(a, b):
    return lax.dot_general(a, b, (((1,), (1,)), ((), ())), preferred_element_type=F32)


def exact(a, b):
    return jnp.dot(a, b, precision=lax.Precision.HIGHEST, preferred_element_type=F32)


def exact_nt(a, b):
    return lax.dot_general(
        a, b, (((1,), (1,)), ((), ())), precision=lax.Precision.HIGHEST, preferred_element_type=F32
    )


def kernel(
    sizes, u_hbm, pot_hbm, rows_d, rows_e,
    u_v, ut, appl, hx, hy, hz, zs, xc, potv, pott, at, ez, bt, bg, pz,
    c_in, c_z, c_y, c_x, c_out, h_in, h_z, h_y, h_x, h_out, mat, linv, linvt,
    load_sem, x_send, x_recv, y_send, y_recv, z_send, z_recv, ar_send, ar_recv,
):
    size = dict(zip(AXES, sizes))
    me = {name: lax.axis_index(name) for name in AXES}
    gx, gy, gz = me["gx"], me["gy"], me["gz"]
    nx, ny, nz = sizes
    ncell = float(nx * ny * nz * CX * CY * CZ)

    per = CY // LOADS
    loads = []
    for i in range(LOADS):
        span = pl.ds(i * per, per)
        loads.append(pltpu.make_async_copy(u_hbm.at[:, span], u_v.at[:, span], load_sem.at[i]))
        loads[-1].start()
    pot_load = pltpu.make_async_copy(pot_hbm, potv, load_sem.at[LOADS])
    pot_load.start()

    barrier = pltpu.get_barrier_semaphore()
    for axis in AXES:
        for off in range(1, size[axis]):
            peer = lax.rem(me[axis] + off, size[axis])
            pl.semaphore_signal(barrier, inc=1, device_id=place(axis, peer), device_id_type=MESH)

    def send(src, dst, ssem, rsem, axis, peer):
        return pltpu.make_async_remote_copy(
            src_ref=src, dst_ref=dst, send_sem=ssem, recv_sem=rsem,
            device_id=place(axis, peer), device_id_type=MESH,
        )

    def x_copy(side, start, count, slot):
        layers = pl.ds(CX - 2, 2) if side == 0 else pl.ds(0, 2)
        span = pl.ds(start, count)
        peer = lax.rem(gx + 1, nx) if side == 0 else lax.rem(gx + nx - 1, nx)
        return send(
            u_hbm.at[layers, span], hx.at[side, :, span],
            x_send.at[side, slot], x_recv.at[side, slot], "gx", peer,
        )

    early_n, late_n = HALF // PIECES, HALF // LATE

    def x_early(side, i):
        return x_copy(side, (HALF if side == 0 else 0) + i * early_n, early_n, i)

    def x_late(side, i):
        return x_copy(side, (0 if side == 0 else HALF) + i * late_n, late_n, PIECES + i)

    def y_copy(side):
        layers = pl.ds(CY - 2, 2) if side == 0 else pl.ds(0, 2)
        peer = lax.rem(gy + 1, ny) if side == 0 else lax.rem(gy + ny - 1, ny)
        return send(
            u_hbm.at[:, layers], hy.at[side], y_send.at[side], y_recv.at[side], "gy", peer
        )

    def z_copy(side, i):
        span = pl.ds(i * (CY // ZPIECES), CY // ZPIECES)
        peer = lax.rem(gz + 1, nz) if side == 0 else lax.rem(gz + nz - 1, nz)
        return send(
            zs.at[span, side], hz.at[span, side],
            z_send.at[side, i], z_recv.at[side, i], "gz", peer,
        )

    def sends(axis, side):
        return me[axis] < size[axis] - 1 if side == 0 else me[axis] > 0

    def receives(axis, side):
        return me[axis] > 0 if side == 0 else me[axis] < size[axis] - 1

    for side in range(2):
        @pl.when(jnp.logical_not(receives("gx", side)))
        def _():
            def clear(y, carry):
                hx[side, :, y] = jnp.zeros((2, CZ, NV), BF16)
                return carry
            lax.fori_loop(0, CY, clear, 0)

        @pl.when(jnp.logical_not(receives("gy", side)))
        def _():
            hy[side] = jnp.zeros((CX, 2, CZ, NV), BF16)

        @pl.when(jnp.logical_not(receives("gz", side)))
        def _():
            def clear(y, carry):
                hz[y, side] = jnp.zeros((2 * CX, NV), BF16)
                return carry
            lax.fori_loop(0, CY, clear, 0)

    r, c = iota((CELLS, CELLS), 0), iota((CELLS, CELLS), 1)
    same_x, same_z = (r >> 5) == (c >> 5), (r & 31) == (c & 31)
    along_z = jnp.where(same_x, tap(jnp.abs((r & 31) - (c & 31))), 0.0)
    along_x = jnp.where(same_z, tap(jnp.abs((r >> 5) - (c >> 5))), 0.0)
    at[...] = (along_x + along_z - jnp.where(r == c, 90.0, 0.0)).astype(BF16)

    r, c = iota((NV, CELLS), 0), iota((NV, CELLS), 1)
    k, x = (r >> 5) & 1, c >> 5
    dist = jnp.where(r < 64, x + 2 - k, CX + k - x)
    bt[...] = jnp.where((r & 31) == (c & 31), tap(dist), 0.0).astype(BF16)

    r, c = iota((2 * CELLS, NV), 0), iota((2 * CELLS, NV), 1)
    k, x = (c >> 5) & 1, (r >> 5) & 7
    dist = jnp.where(c < 64, CX + k - x, x + 2 - k)
    keep = ((r & 31) == (c & 31)) & ((r < CELLS) == (c < 64))
    bg[...] = jnp.where(keep, 2.0 * tap(dist), 0.0).astype(BF16)

    r, c = iota((4 * CX, CELLS), 0), iota((4 * CX, CELLS), 1)
    k, z = r & 1, c & 31
    dist = jnp.where(r < 16, z + 2 - k, CZ + k - z)
    ez[...] = jnp.where(((r >> 1) & 7) == (c >> 5), tap(dist), 0.0).astype(BF16)

    target = jnp.where(r < 16, CZ - 2, 0) + k
    pz[...] = jnp.where((((r >> 1) & 7) == (c >> 5)) & (z == target), 1.0, 0.0).astype(BF16)

    c_in[...] = jnp.zeros_like(c_in)
    h_in[...] = jnp.zeros_like(h_in)

    def add_to(total, value):
        rows = NV // nz
        total[...] += value.reshape(nz, rows, NV)

    def turn(i, carry):
        part = None
        for j in range(4):
            y = i * 4 + j
            block = u_v[:, y].reshape(CELLS, NV)
            turned = block.T
            ut[y + 2] = turned
            both = dot_nn(jnp.concatenate([turned, pz[...]], axis=0), block)
            zs[y] = both[NV:].astype(BF16).reshape(2, 2 * CX, NV)
            part = both[:NV] if part is None else part + both[:NV]
        add_to(c_in, part)
        return carry

    for i in range(LOADS):
        loads[i].wait()
        lax.fori_loop(i * per // 4, (i + 1) * per // 4, turn, 0)
        if i == 0:
            pl.semaphore_wait(barrier, nx + ny + nz - 3)
            for side in range(2):
                @pl.when(sends("gy", side))
                def _():
                    y_copy(side).start()
            for n in range(PIECES):
                for side in range(2):
                    @pl.when(sends("gx", side))
                    def _():
                        x_early(side, n).start()
        if (i + 1) % (LOADS // ZPIECES) == 0:
            for side in range(2):
                @pl.when(sends("gz", side))
                def _():
                    z_copy(side, i // (LOADS // ZPIECES)).start()

    def exchange(stage, axis, source, target):
        for off in range(1, size[axis]):
            peer = lax.rem(me[axis] + off, size[axis])
            send(source(peer), target, ar_send.at[stage], ar_recv.at[stage], axis, peer).start()

    def finish(stage, axis, like):
        whole = like.at[pl.ds(0, size[axis] - 1)]
        pltpu.make_async_copy(whole, whole, ar_recv.at[stage]).wait()
        pltpu.make_async_copy(whole, whole, ar_send.at[stage]).wait()

    def total(ref, count):
        out = ref[0]
        for i in range(1, count):
            out = out + ref[i]
        return out

    def stage0(base, source, z):
        exchange(base, "gz", lambda peer: source.at[peer], z.at[gz])
        z[gz] = source[gz]

    def stage1(base, z, y):
        finish(base, "gz", z)
        y[gy] = total(z, nz)
        exchange(base + 1, "gy", lambda peer: y.at[gy], y.at[gy])

    def stage2(base, y, x):
        finish(base + 1, "gy", y)
        x[gx] = total(y, ny)
        exchange(base + 2, "gx", lambda peer: x.at[gx], x.at[gx])

    def stage3(base, x, out):
        finish(base + 2, "gx", x)
        out[gz] = total(x, nx)
        exchange(base + 3, "gz", lambda peer: out.at[gz], out.at[gz])

    stage0(0, c_in, c_z)

    pot_load.wait()
    pott[...] = potv[...].reshape(CELLS, CY).T * -24.0

    for side in range(2):
        @pl.when(receives("gy", side))
        def _():
            y_copy(side).wait_recv()
        for k in range(2):
            ut[(0 if side == 0 else CY + 2) + k] = hy[side, :, k].reshape(CELLS, NV).T

    def apply(i, carry):
        first = i * STACK
        halo = jnp.concatenate(
            [hz[first + j].reshape(4 * CX, NV).T for j in range(STACK)], axis=0
        )
        acc = dot_nn(ut[pl.ds(first + 2, STACK)].reshape(STACK * NV, CELLS), at[...])
        acc = acc + dot_nn(halo, ez[...])
        part = None
        for j in range(STACK):
            y = first + j
            own = ut[y + 2]
            near = ut[y + 1].astype(F32) + ut[y + 3].astype(F32)
            far = ut[y].astype(F32) + ut[y + 4].astype(F32)
            value = acc[j * NV : (j + 1) * NV] + (16.0 * near - far)
            value = value + pott[pl.ds(y, 1), :] * own.astype(F32)
            appl[y] = value
            term = dot_nt(own, value.astype(BF16))
            part = term if part is None else part + term
        add_to(h_in, part)
        return carry

    groups = CY // ZPIECES // STACK
    for i in range(ZPIECES):
        for side in range(2):
            @pl.when(receives("gz", side))
            def _():
                z_copy(side, i).wait_recv()
        lax.fori_loop(i * groups, (i + 1) * groups, apply, 0)
        if i == 0:
            stage1(0, c_z, c_y)
    stage2(0, c_y, c_x)

    def cross(i, carry):
        span = pl.ds(i * STACK, STACK)
        high = ut[pl.ds(i * STACK + 2, STACK)].reshape(STACK * NV, CELLS)
        low = ut[pl.ds(i * STACK + 2 + HALF, STACK)].reshape(STACK * NV, CELLS)
        both = dot_nn(high, bg[:CELLS]) + dot_nn(low, bg[CELLS:])
        xc[span] = both.astype(BF16).reshape(STACK, NV, NV)
        return carry

    lax.fori_loop(0, HALF // STACK, cross, 0)
    stage3(0, c_x, c_out)

    for i in range(PIECES):
        for side in range(2):
            @pl.when(receives("gx", side))
            def _():
                x_early(side, i).wait_recv()
        part = None
        for j in range(early_n):
            p = i * early_n + j
            layers = jnp.concatenate(
                [hx[1, :, p].reshape(2 * CZ, NV), hx[0, :, p + HALF].reshape(2 * CZ, NV)], axis=0
            )
            term = dot_nn(xc[p], layers)
            part = term if part is None else part + term
        add_to(h_in, part)

    stage0(4, h_in, h_z)
    for i in range(LATE):
        for side in range(2):
            @pl.when(sends("gx", side))
            def _():
                x_late(side, i).start()

    finish(3, "gz", c_out)
    mat[...] = c_out[...].reshape(NV, NV) * (1.0 / ncell)

    prow, plane = iota((8, NV), 0), iota((8, NV), 1)
    outside = iota((NV, NV), 1) >= 8

    def spread(x, s):
        return jnp.broadcast_to(x[s : s + 1, :], (8, NV))

    def split(x):
        a = x.astype(BF16).astype(F32)
        b = (x - a).astype(BF16).astype(F32)
        return a, b, x - a - b

    def eliminate(b, carry):
        panel = mat[0:8, :]
        column = [jnp.broadcast_to(panel[:, s : s + 1], (8, NV)) for s in range(8)]
        inverse = jnp.zeros((8, NV), F32)
        for s in range(8):
            below = prow > s
            scale = 1.0 / spread(column[s], s)
            factor = jnp.where(below, column[s] * scale, 0.0)
            inverse = jnp.where(prow == s, scale, inverse)
            row = jnp.where(plane == s, 1.0, spread(panel, s))
            panel = jnp.where(below & (plane == s), 0.0, panel) - factor * row
            for t in range(s + 1, 8):
                column[t] = column[t] - factor * spread(column[t], s)
        left = jnp.where((plane >= 8) & (plane < NV - 8 * b), panel, 0.0)
        unit = jnp.where(plane < prow, panel, jnp.where(plane == prow, 1.0, 0.0))
        right = jnp.where(plane < 8, unit, panel) * inverse
        p0, p1, p2 = split(left)
        q0, q1, q2 = split(right)
        left = jnp.concatenate([p0, p0, p1, p0, p1, p2], axis=0).T.astype(BF16)
        right = jnp.concatenate([q0, q1, q0, q2, q1, q0], axis=0).astype(BF16)
        rest = jnp.where(outside, mat[...], 0.0) - dot_nn(left, right)
        rest = pltpu.roll(rest, NV - 8, 1)
        mat[0 : NV - 8, :] = rest[8:, :]
        mat[NV - 8 :, :] = pltpu.roll(panel, NV - 8, 1)
        return carry

    lax.fori_loop(0, 5, eliminate, 0)
    stage1(4, h_z, h_y)
    lax.fori_loop(5, 10, eliminate, 0)
    stage2(4, h_y, h_x)
    lax.fori_loop(10, 16, eliminate, 0)
    stage3(4, h_x, h_out)

    row_of, lane_of = iota((NV, NV), 0), iota((NV, NV), 1)
    one = jnp.where(row_of == lane_of, 1.0, 0.0)
    done = mat[...]
    diag = jnp.sum(done * one, axis=1, keepdims=True)
    lower = jnp.where(row_of > lane_of, done, one) * lax.rsqrt(diag)
    linv[...] = lower
    linvt[...] = lower.T

    def widen(i, carry):
        first = i * STACK
        halo = jnp.concatenate(
            [hx[:, :, first + j].reshape(NV, NV).T for j in range(STACK)], axis=0
        )
        appl[pl.ds(first, STACK)] += dot_nn(halo, bt[...]).reshape(STACK, NV, CELLS)
        return carry

    for i in range(LATE):
        for side in range(2):
            @pl.when(receives("gx", side))
            def _():
                x_late(side, i).wait_recv()
    lax.fori_loop(0, CY // STACK, widen, 0)

    finish(7, "gz", h_out)
    lower = linv[...]
    hamil = h_out[...].reshape(NV, NV) * (-1.0 / (24.0 * ncell))
    reduced = exact_nt(exact(lower, hamil), lower)
    reduced = 0.5 * (reduced + reduced.T)
    shifted = reduced - one * (jnp.sum(reduced * one) / NV)
    sign = shifted * lax.rsqrt(jnp.full((1, 1), jnp.sum(shifted * shifted) + 1e-06, F32))
    for step in range(FILTER_STEPS):
        square = exact(sign, sign)
        sign = 1.5 * sign - 0.5 * exact(square, sign)
    rot = exact(linvt[...], exact(0.5 * (one - sign), lower))
    rot = (0.5 * (rot + rot.T)).astype(BF16)

    def densities(i, carry):
        for j in range(STACK):
            y = i * STACK + j
            own = ut[y + 2]
            mixed = dot_nn(rot, own)
            rows_d[pl.ds(y, 1), :] = jnp.sum(own.astype(F32) * mixed, axis=0, keepdims=True)
            rows_e[pl.ds(y, 1), :] = jnp.sum(appl[y] * mixed, axis=0, keepdims=True)
        return carry

    lax.fori_loop(0, CY // STACK, densities, 0)

    for side in range(2):
        @pl.when(sends("gx", side))
        def _():
            for i in range(PIECES):
                x_early(side, i).wait_send()
            for i in range(LATE):
                x_late(side, i).wait_send()

        @pl.when(sends("gy", side))
        def _():
            y_copy(side).wait_send()

        @pl.when(sends("gz", side))
        def _():
            for i in range(ZPIECES):
                z_copy(side, i).wait_send()


def to_cells(rows_d, rows_e, density, energy):
    density[...] = (rows_d[...].T * (1.0 / NB)).reshape(CX, CZ, CY)
    energy[...] = (rows_e[...].T * (-1.0 / (24.0 * NB))).reshape(CX, CZ, CY)


def body(subspace, potential):
    sizes = tuple(lax.axis_size(name) for name in AXES)
    nx, ny, nz = sizes
    rows = NV // nz
    vm, dma = pltpu.VMEM, pltpu.SemaphoreType.DMA
    any_space = pl.BlockSpec(memory_space=pltpu.HBM)
    whole = pl.BlockSpec(memory_space=pltpu.VMEM)
    rows_out = jax.ShapeDtypeStruct((CY, CELLS), F32)
    out = jax.ShapeDtypeStruct((CX, CZ, CY), F32)
    reduce_set = [
        vm((nz, rows, NV), F32), vm((nz, rows, NV), F32), vm((ny, rows, NV), F32),
        vm((nx, rows, NV), F32), vm((nz, rows, NV), F32),
    ]
    rows_d, rows_e = pl.pallas_call(
        functools.partial(kernel, sizes),
        out_shape=(rows_out, rows_out),
        in_specs=[any_space, any_space],
        out_specs=(whole, whole),
        scratch_shapes=[
            vm((CX, CY, CZ, NV), BF16),
            vm((CY + 4, NV, CELLS), BF16),
            vm((CY, NV, CELLS), F32),
            vm((2, 2, CY, CZ, NV), BF16),
            vm((2, CX, 2, CZ, NV), BF16),
            vm((CY, 2, 2 * CX, NV), BF16),
            vm((CY, 2, 2 * CX, NV), BF16),
            vm((HALF, NV, NV), BF16),
            vm((CX, CZ, CY), F32),
            vm((CY, CELLS), F32),
            vm((CELLS, CELLS), BF16),
            vm((4 * CX, CELLS), BF16),
            vm((NV, CELLS), BF16),
            vm((2 * CELLS, NV), BF16),
            vm((4 * CX, CELLS), BF16),
            *reduce_set,
            *reduce_set,
            vm((NV, NV), F32),
            vm((NV, NV), F32),
            vm((NV, NV), F32),
            dma((LOADS + 1,)),
            dma((2, PIECES + LATE)),
            dma((2, PIECES + LATE)),
            dma((2,)),
            dma((2,)),
            dma((2, ZPIECES)),
            dma((2, ZPIECES)),
            dma((8,)),
            dma((8,)),
        ],
        compiler_params=pltpu.CompilerParams(
            collective_id=0, has_side_effects=True, vmem_limit_bytes=61 * 1024 * 1024
        ),
    )(subspace, jnp.transpose(potential, (0, 2, 1)))
    density, energy = pl.pallas_call(
        to_cells, out_shape=(out, out), in_specs=[whole, whole], out_specs=(whole, whole)
    )(rows_d, rows_e)
    return jnp.transpose(density, (0, 2, 1)), jnp.transpose(energy, (0, 2, 1))


def solution(mesh):
    return jax.shard_map(
        body,
        mesh=mesh,
        in_specs=(P("gx", "gy", "gz", None), P("gx", "gy", "gz")),
        out_specs=(P("gx", "gy", "gz"), P("gx", "gy", "gz")),
        check_vma=False,
    )
```

```python
import functools

import jax
import jax.numpy as jnp
from jax import lax
from jax.experimental import pallas as pl
from jax.experimental.pallas import tpu as pltpu
from jax.sharding import PartitionSpec as P

NB = 64
FILTER_STEPS = 8
MESH = pl.DeviceIdType.MESH
AXES = ("gx", "gy", "gz")
F32, BF16 = jnp.float32, jnp.bfloat16

CX, CY, CZ, NV = 8, 48, 32, 128
CELLS = CX * CZ
HALF = CY // 2
LOADS = 2
PIECES = 4
LATE = 3
ZPIECES = 2
STACK = 16


def place(axis, index):
    return tuple(index if name == axis else lax.axis_index(name) for name in AXES)


def iota(shape, dim):
    return lax.broadcasted_iota(jnp.int32, shape, dim)


def tap(distance):
    return jnp.where(distance == 1, 16.0, 0.0) - jnp.where(distance == 2, 1.0, 0.0)


def dot_nn(a, b):
    return jnp.dot(a, b, preferred_element_type=F32)


def dot_nt(a, b):
    return lax.dot_general(a, b, (((1,), (1,)), ((), ())), preferred_element_type=F32)


def exact(a, b):
    return jnp.dot(a, b, precision=lax.Precision.HIGHEST, preferred_element_type=F32)


def three(a, b):
    a0, b0 = a.astype(BF16), b.astype(BF16)
    a1, b1 = (a - a0.astype(F32)).astype(BF16), (b - b0.astype(F32)).astype(BF16)
    return dot_nn(jnp.concatenate([a0, a0, a1], axis=1), jnp.concatenate([b0, b1, b0], axis=0))


def exact_nt(a, b):
    return lax.dot_general(
        a, b, (((1,), (1,)), ((), ())), precision=lax.Precision.HIGHEST, preferred_element_type=F32
    )


def kernel(
    sizes, u_hbm, pot_hbm, rows_d, rows_e,
    u_v, ut, appl, rounded, hx, hy, hz, zs, xc, potv, pott, at, ez, bt, bg, pz,
    total_c, c_in, c_part, c_x, c_out, total_h, h_in, h_part, h_x, h_out, mat, linv, linvt,
    load_sem, x_send, x_recv, y_send, y_recv, z_send, z_recv, ar_send, ar_recv,
):
    size = dict(zip(AXES, sizes))
    me = {name: lax.axis_index(name) for name in AXES}
    gx, gy, gz = me["gx"], me["gy"], me["gz"]
    nx, ny, nz = sizes
    ncell = float(nx * ny * nz * CX * CY * CZ)

    per = CY // LOADS
    loads = []
    for i in range(LOADS):
        span = pl.ds(i * per, per)
        loads.append(pltpu.make_async_copy(u_hbm.at[:, span], u_v.at[:, span], load_sem.at[i]))
        loads[-1].start()
    pot_load = pltpu.make_async_copy(pot_hbm, potv, load_sem.at[LOADS])
    pot_load.start()

    barrier = pltpu.get_barrier_semaphore()
    rows_of_x = [place("gx", lax.rem(gx + off, nx)) for off in range(1, nx)]
    plane = []
    for off in range(1, ny * nz):
        py, pz_at = lax.rem(gy + off // nz, ny), lax.rem(gz + off % nz, nz)
        plane.append((py * nz + pz_at, (gx, py, pz_at)))
    here = gy * nz + gz
    for peer in rows_of_x + [peer for _, peer in plane]:
        pl.semaphore_signal(barrier, inc=1, device_id=peer, device_id_type=MESH)

    def send(src, dst, ssem, rsem, axis, peer):
        return pltpu.make_async_remote_copy(
            src_ref=src, dst_ref=dst, send_sem=ssem, recv_sem=rsem,
            device_id=place(axis, peer), device_id_type=MESH,
        )

    def x_copy(side, start, count, slot):
        layers = pl.ds(CX - 2, 2) if side == 0 else pl.ds(0, 2)
        span = pl.ds(start, count)
        peer = lax.rem(gx + 1, nx) if side == 0 else lax.rem(gx + nx - 1, nx)
        return send(
            u_hbm.at[layers, span], hx.at[side, :, span],
            x_send.at[side, slot], x_recv.at[side, slot], "gx", peer,
        )

    early_n, late_n = HALF // PIECES, HALF // LATE

    def x_early(side, i):
        return x_copy(side, (HALF if side == 0 else 0) + i * early_n, early_n, i)

    def x_late(side, i):
        return x_copy(side, (0 if side == 0 else HALF) + i * late_n, late_n, PIECES + i)

    def y_copy(side):
        layers = pl.ds(CY - 2, 2) if side == 0 else pl.ds(0, 2)
        peer = lax.rem(gy + 1, ny) if side == 0 else lax.rem(gy + ny - 1, ny)
        return send(
            u_hbm.at[:, layers], hy.at[side], y_send.at[side], y_recv.at[side], "gy", peer
        )

    def z_copy(side, i):
        span = pl.ds(i * (CY // ZPIECES), CY // ZPIECES)
        peer = lax.rem(gz + 1, nz) if side == 0 else lax.rem(gz + nz - 1, nz)
        return send(
            zs.at[span, side], hz.at[span, side],
            z_send.at[side, i], z_recv.at[side, i], "gz", peer,
        )

    def sends(axis, side):
        return me[axis] < size[axis] - 1 if side == 0 else me[axis] > 0

    def receives(axis, side):
        return me[axis] > 0 if side == 0 else me[axis] < size[axis] - 1

    r, c = iota((CELLS, CELLS), 0), iota((CELLS, CELLS), 1)
    same_x, same_z = (r >> 5) == (c >> 5), (r & 31) == (c & 31)
    along_z = jnp.where(same_x, tap(jnp.abs((r & 31) - (c & 31))), 0.0)
    along_x = jnp.where(same_z, tap(jnp.abs((r >> 5) - (c >> 5))), 0.0)
    at[...] = (along_x + along_z - jnp.where(r == c, 90.0, 0.0)).astype(BF16)

    r, c = iota((NV, CELLS), 0), iota((NV, CELLS), 1)
    k, x = (r >> 5) & 1, c >> 5
    dist = jnp.where(r < 64, x + 2 - k, CX + k - x)
    bt[...] = jnp.where((r & 31) == (c & 31), tap(dist), 0.0).astype(BF16)

    r, c = iota((CELLS, NV), 0), iota((CELLS, NV), 1)
    k, x = (c >> 5) & 1, (r >> 5) & 3
    dist = jnp.where(c < 64, CX // 2 + k - x, x + 2 - k)
    keep = ((r & 31) == (c & 31)) & ((r < NV) == (c < 64))
    bg[...] = jnp.where(keep, 2.0 * tap(dist), 0.0).astype(BF16)

    r, c = iota((4 * CX, CELLS), 0), iota((4 * CX, CELLS), 1)
    k, z = r & 1, c & 31
    dist = jnp.where(r < 16, z + 2 - k, CZ + k - z)
    ez[...] = jnp.where(((r >> 1) & 7) == (c >> 5), tap(dist), 0.0).astype(BF16)

    total_c[...] = jnp.zeros_like(total_c)
    total_h[...] = jnp.zeros_like(total_h)

    r, c = iota((4 * CX, CELLS), 0), iota((4 * CX, CELLS), 1)
    target = jnp.where(r < 16, CZ - 2, 0) + (r & 1)
    keep = (((r >> 1) & 7) == (c >> 5)) & ((c & 31) == target)
    pz[...] = jnp.where(keep, 1.0, 0.0).astype(BF16)

    def turn(i, carry):
        part = None
        for j in range(per):
            y = i * per + j
            block = u_v[:, y].reshape(CELLS, NV)
            turned = block.T
            ut[y + 2] = turned
            both = dot_nn(jnp.concatenate([turned, pz[...]], axis=0), block)
            zs[y] = both[NV:].astype(BF16).reshape(2, 2 * CX, NV)
            part = both[:NV] if part is None else part + both[:NV]
        total_c[...] += part
        return carry

    for i in range(LOADS):
        loads[i].wait()
        lax.fori_loop(i, i + 1, turn, 0)
        if i == 0:
            pl.semaphore_wait(barrier, nx + ny * nz - 2)
            for n in range(PIECES - 1):
                for side in range(2):
                    @pl.when(sends("gx", side))
                    def _():
                        x_early(side, n).start()
            for side in range(2):
                @pl.when(sends("gz", side))
                def _():
                    z_copy(side, 0).start()

    slices = ny * nz
    thin = NV // slices

    def total(ref, count):
        parts = [ref[i] for i in range(count)]
        while len(parts) > 1:
            parts = [a + b for a, b in zip(parts[::2], parts[1::2])] + parts[len(parts) & ~1 :]
        return parts[0]

    def post(stage, source, target, peer):
        pltpu.make_async_remote_copy(
            src_ref=source, dst_ref=target, send_sem=ar_send.at[stage], recv_sem=ar_recv.at[stage],
            device_id=peer, device_id_type=MESH,
        ).start()

    def finish(stage, like, count):
        whole = like.at[pl.ds(0, count)]
        pltpu.make_async_copy(whole, whole, ar_recv.at[stage]).wait()
        pltpu.make_async_copy(whole, whole, ar_send.at[stage]).wait()

    def scatter(base, whole, source, part):
        for i in range(slices):
            source[i] = whole[i * thin : (i + 1) * thin, :]
        for there, peer in plane:
            post(base, source.at[there], part.at[here], peer)
        part[here] = source[here]

    def across(base, part, x):
        finish(base, part, slices - 1)
        x[gx] = total(part, slices)
        for peer in rows_of_x:
            post(base + 1, x.at[gx], x.at[gx], peer)

    def gather(base, x, out):
        finish(base + 1, x, nx - 1)
        out[here] = total(x, nx)
        for _, peer in plane:
            post(base + 2, out.at[here], out.at[here], peer)

    def gathered(base, out):
        finish(base + 2, out, slices - 1)
        return jnp.concatenate([out[i] for i in range(slices)], axis=0)

    scatter(0, total_c, c_in, c_part)
    for side in range(2):
        @pl.when(sends("gz", side))
        def _():
            z_copy(side, 1).start()

        @pl.when(sends("gy", side))
        def _():
            y_copy(side).start()

    for side in range(2):
        @pl.when(jnp.logical_not(receives("gx", side)))
        def _():
            def clear(y, carry):
                hx[side, :, y] = jnp.zeros((2, CZ, NV), BF16)
                return carry
            lax.fori_loop(0, CY, clear, 0)

        @pl.when(jnp.logical_not(receives("gy", side)))
        def _():
            hy[side] = jnp.zeros((CX, 2, CZ, NV), BF16)

        @pl.when(jnp.logical_not(receives("gz", side)))
        def _():
            def clear(y, carry):
                hz[y, side] = jnp.zeros((2 * CX, NV), BF16)
                return carry
            lax.fori_loop(0, CY, clear, 0)

    high = ut[2 : HALF + 2, :, NV:].reshape(HALF * NV, NV)
    low = ut[HALF + 2 : CY + 2, :, :NV].reshape(HALF * NV, NV)
    both = dot_nn(jnp.concatenate([high, low], axis=1), bg[...])
    xc[...] = both.astype(BF16).reshape(HALF, NV, NV)

    pot_load.wait()
    pott[...] = potv[...].reshape(CELLS, CY).T * -24.0
    ut[0:2] = jnp.zeros((2, NV, CELLS), BF16)
    ut[CY + 2 : CY + 4] = jnp.zeros((2, NV, CELLS), BF16)

    span = CY // ZPIECES

    def apply(first):
        halo = [hz[first + j].reshape(4 * CX, NV).T for j in range(span)]
        rows = jnp.concatenate(
            [ut[first + 2 : first + 2 + span].reshape(span * NV, CELLS), jnp.concatenate(halo, axis=0)],
            axis=1,
        )
        acc = dot_nn(rows, jnp.concatenate([at[...], ez[...]], axis=0))
        for strip in range(0, NV, 16):
            part = slice(strip, strip + 16)
            cell = [ut[first + j, part, :].astype(F32) for j in range(span + 4)]
            for j in range(span):
                y = first + j
                value = acc[j * NV + strip : j * NV + strip + 16]
                value = value + (16.0 * (cell[j + 1] + cell[j + 3]) - (cell[j] + cell[j + 4]))
                value = value + pott[y : y + 1, :] * cell[j + 2]
                appl[y, part, :] = value
                rounded[y, part, :] = value.astype(BF16)

    def product(cells):
        part = None
        for y in cells:
            term = dot_nt(ut[y + 2], rounded[y])
            part = term if part is None else part + term
        total_h[...] += part

    def z_arrived(i):
        for side in range(2):
            @pl.when(receives("gz", side))
            def _():
                z_copy(side, i).wait_recv()

    z_arrived(0)
    apply(0)
    across(0, c_part, c_x)
    for side in range(2):
        @pl.when(sends("gx", side))
        def _():
            x_early(side, PIECES - 1).start()
    z_arrived(1)
    apply(span)
    product(range(2, span))

    for side in range(2):
        @pl.when(receives("gy", side))
        def _():
            y_copy(side).wait_recv()
    for side, far, near in ((0, 0, 1), (1, CY - 1, CY - 2)):
        first = hy[side, :, 1 - side].reshape(CELLS, NV).T.astype(F32)
        second = hy[side, :, side].reshape(CELLS, NV).T.astype(F32)
        appl[far] += 16.0 * first - second
        appl[near] -= first
        rounded[far] = appl[far].astype(BF16)
        rounded[near] = appl[near].astype(BF16)
    product([0, 1, *range(span, CY)])


    for i in range(PIECES):
        for side in range(2):
            @pl.when(receives("gx", side))
            def _():
                x_early(side, i).wait_recv()
        part = None
        for j in range(early_n):
            p = i * early_n + j
            layers = jnp.concatenate(
                [hx[1, :, p].reshape(2 * CZ, NV), hx[0, :, p + HALF].reshape(2 * CZ, NV)], axis=0
            )
            term = dot_nn(xc[p], layers)
            part = term if part is None else part + term
        total_h[...] += part

    scatter(3, total_h, h_in, h_part)
    for side in range(2):
        @pl.when(sends("gx", side))
        def _():
            for i in range(LATE - 1):
                x_late(side, i).start()

    gather(0, c_x, c_out)

    def widen(late):
        for i in range(2):
            side = i if late else 1 - i
            halo = [hx[side, :, i * HALF + j].reshape(2 * CZ, NV).T for j in range(HALF)]
            taps = bt[side * 2 * CZ : (side + 1) * 2 * CZ, side * NV : (side + 1) * NV]
            more = dot_nn(jnp.concatenate(halo, axis=0), taps).reshape(HALF, NV, NV)
            appl[i * HALF : (i + 1) * HALF, :, side * NV : (side + 1) * NV] += more

    widen(False)
    across(3, h_part, h_x)

    mat[...] = gathered(0, c_out) * (1.0 / ncell)

    prow, lane = iota((8, NV), 0), iota((8, NV), 1)
    outside = iota((NV, NV), 1) >= 8

    def spread(x, s):
        return jnp.broadcast_to(x[s : s + 1, :], (8, NV))

    def split(x):
        a = x.astype(BF16).astype(F32)
        b = (x - a).astype(BF16).astype(F32)
        return a, b, x - a - b

    def eliminate(b, carry):
        panel = mat[0:8, :]
        column = [jnp.broadcast_to(panel[:, s : s + 1], (8, NV)) for s in range(8)]
        inverse = jnp.zeros((8, NV), F32)
        for s in range(8):
            below = prow > s
            scale = 1.0 / spread(column[s], s)
            factor = jnp.where(below, column[s] * scale, 0.0)
            inverse = jnp.where(prow == s, scale, inverse)
            row = jnp.where(lane == s, 1.0, spread(panel, s))
            panel = jnp.where(below & (lane == s), 0.0, panel) - factor * row
            for t in range(s + 1, 8):
                column[t] = column[t] - factor * spread(column[t], s)
        left = jnp.where((lane >= 8) & (lane < NV - 8 * b), panel, 0.0)
        unit = jnp.where(lane < prow, panel, jnp.where(lane == prow, 1.0, 0.0))
        right = jnp.where(lane < 8, unit, panel) * inverse
        p0, p1, p2 = split(left)
        q0, q1, q2 = split(right)
        left = jnp.concatenate([p0, p0, p1, p0, p1, p2], axis=0).T.astype(BF16)
        right = jnp.concatenate([q0, q1, q0, q2, q1, q0], axis=0).astype(BF16)
        rest = jnp.where(outside, mat[...], 0.0) - dot_nn(left, right)
        rest = pltpu.roll(rest, NV - 8, 1)
        mat[0 : NV - 8, :] = rest[8:, :]
        mat[NV - 8 :, :] = pltpu.roll(panel, NV - 8, 1)
        return carry

    lax.fori_loop(0, 9, eliminate, 0)
    gather(3, h_x, h_out)
    for side in range(2):
        @pl.when(sends("gx", side))
        def _():
            x_late(side, LATE - 1).start()
    lax.fori_loop(9, 16, eliminate, 0)

    row_of, lane_of = iota((NV, NV), 0), iota((NV, NV), 1)
    one = jnp.where(row_of == lane_of, 1.0, 0.0)
    done = mat[...]
    diag = jnp.sum(done * one, axis=1, keepdims=True)
    lower = jnp.where(row_of > lane_of, done, one) * lax.rsqrt(diag)
    linv[...] = lower
    linvt[...] = lower.T

    for i in range(LATE):
        for side in range(2):
            @pl.when(receives("gx", side))
            def _():
                x_late(side, i).wait_recv()
    widen(True)

    lower = linv[...]
    hamil = gathered(3, h_out) * (-1.0 / (24.0 * ncell))
    reduced = exact_nt(exact(lower, hamil), lower)
    reduced = 0.5 * (reduced + reduced.T)
    shifted = reduced - one * (jnp.sum(reduced * one) / NV)
    sign = shifted * lax.rsqrt(jnp.full((1, 1), jnp.sum(shifted * shifted) + 1e-06, F32))
    for step in range(FILTER_STEPS):
        square = three(sign, sign)
        sign = 1.5 * sign - 0.5 * three(square, sign)
    rot = exact(linvt[...], exact(0.5 * (one - sign), lower))
    rot = (0.5 * (rot + rot.T)).astype(BF16)

    def densities(i, carry):
        for j in range(STACK):
            y = i * STACK + j
            own = ut[y + 2]
            mixed = dot_nn(rot, own)
            rows_d[pl.ds(y, 1), :] = jnp.sum(own.astype(F32) * mixed, axis=0, keepdims=True)
            rows_e[pl.ds(y, 1), :] = jnp.sum(appl[y] * mixed, axis=0, keepdims=True)
        return carry

    lax.fori_loop(0, CY // STACK, densities, 0)

    for side in range(2):
        @pl.when(sends("gx", side))
        def _():
            for i in range(PIECES):
                x_early(side, i).wait_send()
            for i in range(LATE):
                x_late(side, i).wait_send()

        @pl.when(sends("gy", side))
        def _():
            y_copy(side).wait_send()

        @pl.when(sends("gz", side))
        def _():
            for i in range(ZPIECES):
                z_copy(side, i).wait_send()


def to_cells(rows_d, rows_e, density, energy):
    density[...] = (rows_d[...].T * (1.0 / NB)).reshape(CX, CZ, CY)
    energy[...] = (rows_e[...].T * (-1.0 / (24.0 * NB))).reshape(CX, CZ, CY)


def body(subspace, potential):
    sizes = tuple(lax.axis_size(name) for name in AXES)
    nx, ny, nz = sizes
    vm, dma = pltpu.VMEM, pltpu.SemaphoreType.DMA
    any_space = pl.BlockSpec(memory_space=pltpu.HBM)
    whole = pl.BlockSpec(memory_space=pltpu.VMEM)
    rows_out = jax.ShapeDtypeStruct((CY, CELLS), F32)
    out = jax.ShapeDtypeStruct((CX, CZ, CY), F32)
    slices = ny * nz
    thin = NV // slices
    reduce_set = [
        vm((NV, NV), F32),
        vm((slices, thin, NV), F32), vm((slices, thin, NV), F32),
        vm((nx, thin, NV), F32), vm((slices, thin, NV), F32),
    ]
    rows_d, rows_e = pl.pallas_call(
        functools.partial(kernel, sizes),
        out_shape=(rows_out, rows_out),
        in_specs=[any_space, any_space],
        out_specs=(whole, whole),
        scratch_shapes=[
            vm((CX, CY, CZ, NV), BF16),
            vm((CY + 4, NV, CELLS), BF16),
            vm((CY, NV, CELLS), F32),
            vm((CY, NV, CELLS), BF16),
            vm((2, 2, CY, CZ, NV), BF16),
            vm((2, CX, 2, CZ, NV), BF16),
            vm((CY, 2, 2 * CX, NV), BF16),
            vm((CY, 2, 2 * CX, NV), BF16),
            vm((HALF, NV, NV), BF16),
            vm((CX, CZ, CY), F32),
            vm((CY, CELLS), F32),
            vm((CELLS, CELLS), BF16),
            vm((4 * CX, CELLS), BF16),
            vm((NV, CELLS), BF16),
            vm((CELLS, NV), BF16),
            vm((4 * CX, CELLS), BF16),
            *reduce_set,
            *reduce_set,
            vm((NV, NV), F32),
            vm((NV, NV), F32),
            vm((NV, NV), F32),
            dma((LOADS + 1,)),
            dma((2, PIECES + LATE)),
            dma((2, PIECES + LATE)),
            dma((2,)),
            dma((2,)),
            dma((2, ZPIECES)),
            dma((2, ZPIECES)),
            dma((6,)),
            dma((6,)),
        ],
        compiler_params=pltpu.CompilerParams(
            collective_id=0, has_side_effects=True, vmem_limit_bytes=61 * 1024 * 1024
        ),
    )(subspace, jnp.transpose(potential, (0, 2, 1)))
    density, energy = pl.pallas_call(
        to_cells, out_shape=(out, out), in_specs=[whole, whole], out_specs=(whole, whole)
    )(rows_d, rows_e)
    return jnp.transpose(density, (0, 2, 1)), jnp.transpose(energy, (0, 2, 1))


def solution(mesh):
    return jax.shard_map(
        body,
        mesh=mesh,
        in_specs=(P("gx", "gy", "gz", None), P("gx", "gy", "gz")),
        out_specs=(P("gx", "gy", "gz"), P("gx", "gy", "gz")),
        check_vma=False,
    )
```

```python
import functools

import jax
import jax.numpy as jnp
from jax import lax
from jax.experimental import pallas as pl
from jax.experimental.pallas import tpu as pltpu
from jax.sharding import PartitionSpec as P

NB = 64
FILTER_STEPS = 8
MESH = pl.DeviceIdType.MESH
AXES = ("gx", "gy", "gz")
F32, BF16 = jnp.float32, jnp.bfloat16

CX, CY, CZ, NV = 8, 48, 32, 128
CELLS = CX * CZ
HALF = CY // 2
LOADS = 2
PIECES = 4
LATE = 4
ZPIECES = 2
STACK = 16


def place(axis, index):
    return tuple(index if name == axis else lax.axis_index(name) for name in AXES)


def iota(shape, dim):
    return lax.broadcasted_iota(jnp.int32, shape, dim)


def tap(distance):
    return jnp.where(distance == 1, 16.0, 0.0) - jnp.where(distance == 2, 1.0, 0.0)


def dot_nn(a, b):
    return jnp.dot(a, b, preferred_element_type=F32)


def dot_nt(a, b):
    return lax.dot_general(a, b, (((1,), (1,)), ((), ())), preferred_element_type=F32)


def exact(a, b):
    return jnp.dot(a, b, precision=lax.Precision.HIGHEST, preferred_element_type=F32)


def three(a, b):
    a0, b0 = a.astype(BF16), b.astype(BF16)
    a1, b1 = (a - a0.astype(F32)).astype(BF16), (b - b0.astype(F32)).astype(BF16)
    return dot_nn(jnp.concatenate([a0, a0, a1], axis=1), jnp.concatenate([b0, b1, b0], axis=0))


def exact_nt(a, b):
    return lax.dot_general(
        a, b, (((1,), (1,)), ((), ())), precision=lax.Precision.HIGHEST, preferred_element_type=F32
    )


def kernel(
    sizes, u_hbm, pot_hbm, rows_d, rows_e,
    u_v, ut, appl, rounded, hx, hy, hz, zs, xc, potv, pott, at, ez, bt, bg, pz,
    total_c, c_in, c_part, c_x, c_out, total_h, h_in, h_part, h_x, h_out, mat, linv, linvt,
    load_sem, x_send, x_recv, y_send, y_recv, z_send, z_recv, ar_send, ar_recv,
):
    size = dict(zip(AXES, sizes))
    me = {name: lax.axis_index(name) for name in AXES}
    gx, gy, gz = me["gx"], me["gy"], me["gz"]
    nx, ny, nz = sizes
    ncell = float(nx * ny * nz * CX * CY * CZ)

    per = CY // LOADS
    loads = []
    for i in range(LOADS):
        span = pl.ds(i * per, per)
        loads.append(pltpu.make_async_copy(u_hbm.at[:, span], u_v.at[:, span], load_sem.at[i]))
        loads[-1].start()
    pot_load = pltpu.make_async_copy(pot_hbm, potv, load_sem.at[LOADS])
    pot_load.start()

    barrier = pltpu.get_barrier_semaphore()
    rows_of_x = [place("gx", lax.rem(gx + off, nx)) for off in range(1, nx)]
    plane = []
    for off in range(1, ny * nz):
        py, pz_at = lax.rem(gy + off // nz, ny), lax.rem(gz + off % nz, nz)
        plane.append((py * nz + pz_at, (gx, py, pz_at)))
    here = gy * nz + gz
    for peer in rows_of_x + [peer for _, peer in plane]:
        pl.semaphore_signal(barrier, inc=1, device_id=peer, device_id_type=MESH)

    def send(src, dst, ssem, rsem, axis, peer):
        return pltpu.make_async_remote_copy(
            src_ref=src, dst_ref=dst, send_sem=ssem, recv_sem=rsem,
            device_id=place(axis, peer), device_id_type=MESH,
        )

    def x_copy(side, start, count, slot):
        layers = pl.ds(CX - 2, 2) if side == 0 else pl.ds(0, 2)
        span = pl.ds(start, count)
        peer = lax.rem(gx + 1, nx) if side == 0 else lax.rem(gx + nx - 1, nx)
        return send(
            u_hbm.at[layers, span], hx.at[side, :, span],
            x_send.at[side, slot], x_recv.at[side, slot], "gx", peer,
        )

    early_n, late_n = HALF // PIECES, HALF // LATE

    def x_early(side, i):
        return x_copy(side, (HALF if side == 0 else 0) + i * early_n, early_n, i)

    def x_late(side, i):
        return x_copy(side, (0 if side == 0 else HALF) + i * late_n, late_n, PIECES + i)

    def y_copy(side):
        layers = pl.ds(CY - 2, 2) if side == 0 else pl.ds(0, 2)
        peer = lax.rem(gy + 1, ny) if side == 0 else lax.rem(gy + ny - 1, ny)
        return send(
            u_hbm.at[:, layers], hy.at[side], y_send.at[side], y_recv.at[side], "gy", peer
        )

    def z_copy(side, i):
        span = pl.ds(i * (CY // ZPIECES), CY // ZPIECES)
        peer = lax.rem(gz + 1, nz) if side == 0 else lax.rem(gz + nz - 1, nz)
        return send(
            zs.at[span, side], hz.at[span, side],
            z_send.at[side, i], z_recv.at[side, i], "gz", peer,
        )

    def sends(axis, side):
        return me[axis] < size[axis] - 1 if side == 0 else me[axis] > 0

    def receives(axis, side):
        return me[axis] > 0 if side == 0 else me[axis] < size[axis] - 1

    r, c = iota((CELLS, CELLS), 0), iota((CELLS, CELLS), 1)
    same_x, same_z = (r >> 5) == (c >> 5), (r & 31) == (c & 31)
    along_z = jnp.where(same_x, tap(jnp.abs((r & 31) - (c & 31))), 0.0)
    along_x = jnp.where(same_z, tap(jnp.abs((r >> 5) - (c >> 5))), 0.0)
    at[...] = (along_x + along_z - jnp.where(r == c, 90.0, 0.0)).astype(BF16)

    r, c = iota((NV, CELLS), 0), iota((NV, CELLS), 1)
    k, x = (r >> 5) & 1, c >> 5
    dist = jnp.where(r < 64, x + 2 - k, CX + k - x)
    bt[...] = jnp.where((r & 31) == (c & 31), tap(dist), 0.0).astype(BF16)

    r, c = iota((CELLS, NV), 0), iota((CELLS, NV), 1)
    k, x = (c >> 5) & 1, (r >> 5) & 3
    dist = jnp.where(c < 64, CX // 2 + k - x, x + 2 - k)
    keep = ((r & 31) == (c & 31)) & ((r < NV) == (c < 64))
    bg[...] = jnp.where(keep, 2.0 * tap(dist), 0.0).astype(BF16)

    r, c = iota((4 * CX, CELLS), 0), iota((4 * CX, CELLS), 1)
    k, z = r & 1, c & 31
    dist = jnp.where(r < 16, z + 2 - k, CZ + k - z)
    ez[...] = jnp.where(((r >> 1) & 7) == (c >> 5), tap(dist), 0.0).astype(BF16)

    total_c[...] = jnp.zeros_like(total_c)
    total_h[...] = jnp.zeros_like(total_h)

    r, c = iota((4 * CX, CELLS), 0), iota((4 * CX, CELLS), 1)
    target = jnp.where(r < 16, CZ - 2, 0) + (r & 1)
    keep = (((r >> 1) & 7) == (c >> 5)) & ((c & 31) == target)
    pz[...] = jnp.where(keep, 1.0, 0.0).astype(BF16)

    def turn(i, carry):
        part = None
        for j in range(per):
            y = i * per + j
            block = u_v[:, y].reshape(CELLS, NV)
            turned = block.T
            ut[y + 2] = turned
            both = dot_nn(jnp.concatenate([turned, pz[...]], axis=0), block)
            zs[y] = both[NV:].astype(BF16).reshape(2, 2 * CX, NV)
            part = both[:NV] if part is None else part + both[:NV]
        total_c[...] += part
        return carry

    for i in range(LOADS):
        loads[i].wait()
        lax.fori_loop(i, i + 1, turn, 0)

    pl.semaphore_wait(barrier, nx + ny * nz - 2)
    for side in range(2):
        @pl.when(sends("gx", side))
        def _():
            for n in range(PIECES - 1):
                x_early(side, n).start()

        @pl.when(sends("gz", side))
        def _():
            z_copy(side, 0).start()

    slices = ny * nz
    thin = NV // slices

    def total(ref, count):
        parts = [ref[i] for i in range(count)]
        while len(parts) > 1:
            parts = [a + b for a, b in zip(parts[::2], parts[1::2])] + parts[len(parts) & ~1 :]
        return parts[0]

    def post(stage, source, target, peer):
        pltpu.make_async_remote_copy(
            src_ref=source, dst_ref=target, send_sem=ar_send.at[stage], recv_sem=ar_recv.at[stage],
            device_id=peer, device_id_type=MESH,
        ).start()

    def finish(stage, like, count):
        whole = like.at[pl.ds(0, count)]
        pltpu.make_async_copy(whole, whole, ar_recv.at[stage]).wait()
        pltpu.make_async_copy(whole, whole, ar_send.at[stage]).wait()

    def scatter(base, whole, source, part):
        for i in range(slices):
            source[i] = whole[i * thin : (i + 1) * thin, :]
        for there, peer in plane:
            post(base, source.at[there], part.at[here], peer)
        part[here] = source[here]

    def across(base, part, x):
        finish(base, part, slices - 1)
        x[gx] = total(part, slices)
        for peer in rows_of_x:
            post(base + 1, x.at[gx], x.at[gx], peer)

    def gather(base, x, out):
        finish(base + 1, x, nx - 1)
        out[here] = total(x, nx)
        for _, peer in plane:
            post(base + 2, out.at[here], out.at[here], peer)

    def gathered(base, out):
        finish(base + 2, out, slices - 1)
        return jnp.concatenate([out[i] for i in range(slices)], axis=0)

    scatter(0, total_c, c_in, c_part)
    for side in range(2):
        @pl.when(sends("gz", side))
        def _():
            z_copy(side, 1).start()

        @pl.when(sends("gy", side))
        def _():
            y_copy(side).start()

    for side in range(2):
        @pl.when(jnp.logical_not(receives("gx", side)))
        def _():
            def clear(y, carry):
                hx[side, :, y] = jnp.zeros((2, CZ, NV), BF16)
                return carry
            lax.fori_loop(0, CY, clear, 0)

        @pl.when(jnp.logical_not(receives("gy", side)))
        def _():
            hy[side] = jnp.zeros((CX, 2, CZ, NV), BF16)

        @pl.when(jnp.logical_not(receives("gz", side)))
        def _():
            def clear(y, carry):
                hz[y, side] = jnp.zeros((2 * CX, NV), BF16)
                return carry
            lax.fori_loop(0, CY, clear, 0)

    high = ut[2 : HALF + 2, :, NV:].reshape(HALF * NV, NV)
    low = ut[HALF + 2 : CY + 2, :, :NV].reshape(HALF * NV, NV)
    both = dot_nn(jnp.concatenate([high, low], axis=1), bg[...])
    xc[...] = both.astype(BF16).reshape(HALF, NV, NV)

    pot_load.wait()
    pott[...] = potv[...].reshape(CELLS, CY).T * -24.0
    ut[0:2] = jnp.zeros((2, NV, CELLS), BF16)
    ut[CY + 2 : CY + 4] = jnp.zeros((2, NV, CELLS), BF16)

    span = CY // ZPIECES

    def apply(first):
        halo = [hz[first + j].reshape(4 * CX, NV).T for j in range(span)]
        rows = jnp.concatenate(
            [ut[first + 2 : first + 2 + span].reshape(span * NV, CELLS), jnp.concatenate(halo, axis=0)],
            axis=1,
        )
        acc = dot_nn(rows, jnp.concatenate([at[...], ez[...]], axis=0))
        for strip in range(0, NV, 16):
            part = slice(strip, strip + 16)
            cell = [ut[first + j, part, :].astype(F32) for j in range(span + 4)]
            for j in range(span):
                y = first + j
                value = acc[j * NV + strip : j * NV + strip + 16]
                value = value + (16.0 * (cell[j + 1] + cell[j + 3]) - (cell[j] + cell[j + 4]))
                value = value + pott[y : y + 1, :] * cell[j + 2]
                appl[y, part, :] = value
                rounded[y, part, :] = value.astype(BF16)

    def product(cells):
        part = None
        for y in cells:
            term = dot_nt(ut[y + 2], rounded[y])
            part = term if part is None else part + term
        total_h[...] += part

    def z_arrived(i):
        for side in range(2):
            @pl.when(receives("gz", side))
            def _():
                z_copy(side, i).wait_recv()

    z_arrived(0)
    apply(0)
    across(0, c_part, c_x)
    for side in range(2):
        @pl.when(sends("gx", side))
        def _():
            x_early(side, PIECES - 1).start()
    z_arrived(1)
    apply(span)
    product(range(2, span))

    for side in range(2):
        @pl.when(sends("gx", side))
        def _():
            for i in range(LATE - 1):
                x_late(side, i).start()

    for side in range(2):
        @pl.when(receives("gy", side))
        def _():
            y_copy(side).wait_recv()
    for side, far, near in ((0, 0, 1), (1, CY - 1, CY - 2)):
        first = hy[side, :, 1 - side].reshape(CELLS, NV).T.astype(F32)
        second = hy[side, :, side].reshape(CELLS, NV).T.astype(F32)
        appl[far] += 16.0 * first - second
        appl[near] -= first
        rounded[far] = appl[far].astype(BF16)
        rounded[near] = appl[near].astype(BF16)
    product([0, 1, *range(span, CY)])


    for i in range(PIECES):
        for side in range(2):
            @pl.when(receives("gx", side))
            def _():
                x_early(side, i).wait_recv()
        part = None
        for j in range(early_n):
            p = i * early_n + j
            layers = jnp.concatenate(
                [hx[1, :, p].reshape(2 * CZ, NV), hx[0, :, p + HALF].reshape(2 * CZ, NV)], axis=0
            )
            term = dot_nn(xc[p], layers)
            part = term if part is None else part + term
        total_h[...] += part

    scatter(3, total_h, h_in, h_part)

    gather(0, c_x, c_out)

    def widen(late):
        for i in range(2):
            side = i if late else 1 - i
            halo = [hx[side, :, i * HALF + j].reshape(2 * CZ, NV).T for j in range(HALF)]
            taps = bt[side * 2 * CZ : (side + 1) * 2 * CZ, side * NV : (side + 1) * NV]
            more = dot_nn(jnp.concatenate(halo, axis=0), taps).reshape(HALF, NV, NV)
            appl[i * HALF : (i + 1) * HALF, :, side * NV : (side + 1) * NV] += more

    widen(False)
    across(3, h_part, h_x)

    mat[...] = gathered(0, c_out) * (1.0 / ncell)

    prow, lane = iota((8, NV), 0), iota((8, NV), 1)
    outside = iota((NV, NV), 1) >= 8

    def spread(x, s):
        return jnp.broadcast_to(x[s : s + 1, :], (8, NV))

    def split(x):
        a = x.astype(BF16).astype(F32)
        b = (x - a).astype(BF16).astype(F32)
        return a, b, x - a - b

    def eliminate(b, carry):
        panel = mat[0:8, :]
        column = [jnp.broadcast_to(panel[:, s : s + 1], (8, NV)) for s in range(8)]
        inverse = jnp.zeros((8, NV), F32)
        for s in range(8):
            below = prow > s
            scale = 1.0 / spread(column[s], s)
            factor = jnp.where(below, column[s] * scale, 0.0)
            inverse = jnp.where(prow == s, scale, inverse)
            row = jnp.where(lane == s, 1.0, spread(panel, s))
            panel = jnp.where(below & (lane == s), 0.0, panel) - factor * row
            for t in range(s + 1, 8):
                column[t] = column[t] - factor * spread(column[t], s)
        left = jnp.where((lane >= 8) & (lane < NV - 8 * b), panel, 0.0)
        unit = jnp.where(lane < prow, panel, jnp.where(lane == prow, 1.0, 0.0))
        right = jnp.where(lane < 8, unit, panel) * inverse
        p0, p1, p2 = split(left)
        q0, q1, q2 = split(right)
        left = jnp.concatenate([p0, p0, p1, p0, p1, p2], axis=0).T.astype(BF16)
        right = jnp.concatenate([q0, q1, q0, q2, q1, q0], axis=0).astype(BF16)
        rest = jnp.where(outside, mat[...], 0.0) - dot_nn(left, right)
        rest = pltpu.roll(rest, NV - 8, 1)
        mat[0 : NV - 8, :] = rest[8:, :]
        mat[NV - 8 :, :] = pltpu.roll(panel, NV - 8, 1)
        return carry

    lax.fori_loop(0, 8, eliminate, 0)
    gather(3, h_x, h_out)
    for side in range(2):
        @pl.when(sends("gx", side))
        def _():
            x_late(side, LATE - 1).start()
    lax.fori_loop(8, 16, eliminate, 0)

    row_of, lane_of = iota((NV, NV), 0), iota((NV, NV), 1)
    one = jnp.where(row_of == lane_of, 1.0, 0.0)
    done = mat[...]
    diag = jnp.sum(done * one, axis=1, keepdims=True)
    lower = jnp.where(row_of > lane_of, done, one) * lax.rsqrt(diag)
    linv[...] = lower
    linvt[...] = lower.T

    for i in range(LATE):
        for side in range(2):
            @pl.when(receives("gx", side))
            def _():
                x_late(side, i).wait_recv()
    widen(True)

    lower = linv[...]
    hamil = gathered(3, h_out) * (-1.0 / (24.0 * ncell))
    reduced = exact_nt(exact(lower, hamil), lower)
    reduced = 0.5 * (reduced + reduced.T)
    shifted = reduced - one * (jnp.sum(reduced * one) / NV)
    sign = shifted * lax.rsqrt(jnp.full((1, 1), jnp.sum(shifted * shifted) + 1e-06, F32))
    for step in range(FILTER_STEPS):
        square = three(sign, sign)
        sign = 1.5 * sign - 0.5 * three(square, sign)
    rot = exact(linvt[...], exact(0.5 * (one - sign), lower))
    rot = (0.5 * (rot + rot.T)).astype(BF16)

    def densities(i, carry):
        for j in range(STACK):
            y = i * STACK + j
            own = ut[y + 2]
            mixed = dot_nn(rot, own)
            rows_d[pl.ds(y, 1), :] = jnp.sum(own.astype(F32) * mixed, axis=0, keepdims=True)
            rows_e[pl.ds(y, 1), :] = jnp.sum(appl[y] * mixed, axis=0, keepdims=True)
        return carry

    lax.fori_loop(0, CY // STACK, densities, 0)

    for side in range(2):
        @pl.when(sends("gx", side))
        def _():
            for i in range(PIECES):
                x_early(side, i).wait_send()
            for i in range(LATE):
                x_late(side, i).wait_send()

        @pl.when(sends("gy", side))
        def _():
            y_copy(side).wait_send()

        @pl.when(sends("gz", side))
        def _():
            for i in range(ZPIECES):
                z_copy(side, i).wait_send()


def to_cells(rows_d, rows_e, density, energy):
    density[...] = (rows_d[...].T * (1.0 / NB)).reshape(CX, CZ, CY)
    energy[...] = (rows_e[...].T * (-1.0 / (24.0 * NB))).reshape(CX, CZ, CY)


def body(subspace, potential):
    sizes = tuple(lax.axis_size(name) for name in AXES)
    nx, ny, nz = sizes
    vm, dma = pltpu.VMEM, pltpu.SemaphoreType.DMA
    any_space = pl.BlockSpec(memory_space=pltpu.HBM)
    whole = pl.BlockSpec(memory_space=pltpu.VMEM)
    rows_out = jax.ShapeDtypeStruct((CY, CELLS), F32)
    out = jax.ShapeDtypeStruct((CX, CZ, CY), F32)
    slices = ny * nz
    thin = NV // slices
    reduce_set = [
        vm((NV, NV), F32),
        vm((slices, thin, NV), F32), vm((slices, thin, NV), F32),
        vm((nx, thin, NV), F32), vm((slices, thin, NV), F32),
    ]
    rows_d, rows_e = pl.pallas_call(
        functools.partial(kernel, sizes),
        out_shape=(rows_out, rows_out),
        in_specs=[any_space, any_space],
        out_specs=(whole, whole),
        scratch_shapes=[
            vm((CX, CY, CZ, NV), BF16),
            vm((CY + 4, NV, CELLS), BF16),
            vm((CY, NV, CELLS), F32),
            vm((CY, NV, CELLS), BF16),
            vm((2, 2, CY, CZ, NV), BF16),
            vm((2, CX, 2, CZ, NV), BF16),
            vm((CY, 2, 2 * CX, NV), BF16),
            vm((CY, 2, 2 * CX, NV), BF16),
            vm((HALF, NV, NV), BF16),
            vm((CX, CZ, CY), F32),
            vm((CY, CELLS), F32),
            vm((CELLS, CELLS), BF16),
            vm((4 * CX, CELLS), BF16),
            vm((NV, CELLS), BF16),
            vm((CELLS, NV), BF16),
            vm((4 * CX, CELLS), BF16),
            *reduce_set,
            *reduce_set,
            vm((NV, NV), F32),
            vm((NV, NV), F32),
            vm((NV, NV), F32),
            dma((LOADS + 1,)),
            dma((2, PIECES + LATE)),
            dma((2, PIECES + LATE)),
            dma((2,)),
            dma((2,)),
            dma((2, ZPIECES)),
            dma((2, ZPIECES)),
            dma((6,)),
            dma((6,)),
        ],
        compiler_params=pltpu.CompilerParams(
            collective_id=0, has_side_effects=True, vmem_limit_bytes=55072 * 1024
        ),
    )(subspace, jnp.transpose(potential, (0, 2, 1)))
    density, energy = pl.pallas_call(
        to_cells,
        out_shape=(out, out),
        in_specs=[whole, whole],
        out_specs=(whole, whole),
        compiler_params=pltpu.CompilerParams(vmem_limit_bytes=8 * 1024 * 1024),
    )(rows_d, rows_e)
    return jnp.transpose(density, (0, 2, 1)), jnp.transpose(energy, (0, 2, 1))


def solution(mesh):
    return jax.shard_map(
        body,
        mesh=mesh,
        in_specs=(P("gx", "gy", "gz", None), P("gx", "gy", "gz")),
        out_specs=(P("gx", "gy", "gz"), P("gx", "gy", "gz")),
        check_vma=False,
    )
```

```python
import functools

import jax
import jax.numpy as jnp
from jax import lax
from jax.experimental import pallas as pl
from jax.experimental.pallas import tpu as pltpu
from jax.sharding import PartitionSpec as P

NB = 64
FILTER_STEPS = 8
MESH = pl.DeviceIdType.MESH
AXES = ("gx", "gy", "gz")
F32, BF16 = jnp.float32, jnp.bfloat16

CX, CY, CZ, NV = 8, 48, 32, 128
CELLS = CX * CZ
HALF = CY // 2
LOADS = 2
PIECES = 4
LATE = 8
LAST = 2
ZPIECES = 2
STACK = 16


def place(axis, index):
    return tuple(index if name == axis else lax.axis_index(name) for name in AXES)


def iota(shape, dim):
    return lax.broadcasted_iota(jnp.int32, shape, dim)


def tap(distance):
    return jnp.where(distance == 1, 16.0, 0.0) - jnp.where(distance == 2, 1.0, 0.0)


def dot_nn(a, b):
    return jnp.dot(a, b, preferred_element_type=F32)


def dot_nt(a, b):
    return lax.dot_general(a, b, (((1,), (1,)), ((), ())), preferred_element_type=F32)


def exact(a, b):
    return jnp.dot(a, b, precision=lax.Precision.HIGHEST, preferred_element_type=F32)


def three(a, b):
    a0, b0 = a.astype(BF16), b.astype(BF16)
    a1, b1 = (a - a0.astype(F32)).astype(BF16), (b - b0.astype(F32)).astype(BF16)
    return dot_nn(jnp.concatenate([a0, a0, a1], axis=1), jnp.concatenate([b0, b1, b0], axis=0))


def exact_nt(a, b):
    return lax.dot_general(
        a, b, (((1,), (1,)), ((), ())), precision=lax.Precision.HIGHEST, preferred_element_type=F32
    )


def kernel(
    sizes, u_hbm, pot_hbm, rows_d, rows_e,
    u_v, ut, appl, rounded, hx, hy, hz, zs, xc, potv, pott, at, ez, bt, bg, pz,
    total_c, c_in, c_part, c_x, c_out, total_h, h_in, h_part, h_x, h_out, mat, linv, linvt,
    load_sem, x_send, x_recv, y_send, y_recv, z_send, z_recv, ar_send, ar_recv,
):
    size = dict(zip(AXES, sizes))
    me = {name: lax.axis_index(name) for name in AXES}
    gx, gy, gz = me["gx"], me["gy"], me["gz"]
    nx, ny, nz = sizes
    ncell = float(nx * ny * nz * CX * CY * CZ)

    per = CY // LOADS
    loads = []
    for i in range(LOADS):
        span = pl.ds(i * per, per)
        loads.append(pltpu.make_async_copy(u_hbm.at[:, span], u_v.at[:, span], load_sem.at[i]))
        loads[-1].start()
    pot_load = pltpu.make_async_copy(pot_hbm, potv, load_sem.at[LOADS])
    pot_load.start()

    barrier = pltpu.get_barrier_semaphore()
    rows_of_x = [place("gx", lax.rem(gx + off, nx)) for off in range(1, nx)]
    plane = []
    for off in range(1, ny * nz):
        py, pz_at = lax.rem(gy + off // nz, ny), lax.rem(gz + off % nz, nz)
        plane.append((py * nz + pz_at, (gx, py, pz_at)))
    here = gy * nz + gz
    for peer in rows_of_x + [peer for _, peer in plane]:
        pl.semaphore_signal(barrier, inc=1, device_id=peer, device_id_type=MESH)

    def send(src, dst, ssem, rsem, axis, peer):
        return pltpu.make_async_remote_copy(
            src_ref=src, dst_ref=dst, send_sem=ssem, recv_sem=rsem,
            device_id=place(axis, peer), device_id_type=MESH,
        )

    def x_copy(side, start, count, slot):
        layers = pl.ds(CX - 2, 2) if side == 0 else pl.ds(0, 2)
        span = pl.ds(start, count)
        peer = lax.rem(gx + 1, nx) if side == 0 else lax.rem(gx + nx - 1, nx)
        return send(
            u_hbm.at[layers, span], hx.at[side, :, span],
            x_send.at[side, slot], x_recv.at[side, slot], "gx", peer,
        )

    early_n, late_n = HALF // PIECES, HALF // LATE

    def x_early(side, i):
        return x_copy(side, (HALF if side == 0 else 0) + i * early_n, early_n, i)

    def x_late(side, i):
        return x_copy(side, (0 if side == 0 else HALF) + i * late_n, late_n, PIECES + i)

    def y_copy(side):
        layers = pl.ds(CY - 2, 2) if side == 0 else pl.ds(0, 2)
        peer = lax.rem(gy + 1, ny) if side == 0 else lax.rem(gy + ny - 1, ny)
        return send(
            u_hbm.at[:, layers], hy.at[side], y_send.at[side], y_recv.at[side], "gy", peer
        )

    def z_copy(side, i):
        span = pl.ds(i * (CY // ZPIECES), CY // ZPIECES)
        peer = lax.rem(gz + 1, nz) if side == 0 else lax.rem(gz + nz - 1, nz)
        return send(
            zs.at[span, side], hz.at[span, side],
            z_send.at[side, i], z_recv.at[side, i], "gz", peer,
        )

    def sends(axis, side):
        return me[axis] < size[axis] - 1 if side == 0 else me[axis] > 0

    def receives(axis, side):
        return me[axis] > 0 if side == 0 else me[axis] < size[axis] - 1

    r, c = iota((CELLS, CELLS), 0), iota((CELLS, CELLS), 1)
    same_x, same_z = (r >> 5) == (c >> 5), (r & 31) == (c & 31)
    along_z = jnp.where(same_x, tap(jnp.abs((r & 31) - (c & 31))), 0.0)
    along_x = jnp.where(same_z, tap(jnp.abs((r >> 5) - (c >> 5))), 0.0)
    at[...] = (along_x + along_z - jnp.where(r == c, 90.0, 0.0)).astype(BF16)

    r, c = iota((NV, CELLS), 0), iota((NV, CELLS), 1)
    k, x = (r >> 5) & 1, c >> 5
    dist = jnp.where(r < 64, x + 2 - k, CX + k - x)
    bt[...] = jnp.where((r & 31) == (c & 31), tap(dist), 0.0).astype(BF16)

    r, c = iota((CELLS, NV), 0), iota((CELLS, NV), 1)
    k, x = (c >> 5) & 1, (r >> 5) & 3
    dist = jnp.where(c < 64, CX // 2 + k - x, x + 2 - k)
    keep = ((r & 31) == (c & 31)) & ((r < NV) == (c < 64))
    bg[...] = jnp.where(keep, 2.0 * tap(dist), 0.0).astype(BF16)

    r, c = iota((4 * CX, CELLS), 0), iota((4 * CX, CELLS), 1)
    k, z = r & 1, c & 31
    dist = jnp.where(r < 16, z + 2 - k, CZ + k - z)
    ez[...] = jnp.where(((r >> 1) & 7) == (c >> 5), tap(dist), 0.0).astype(BF16)

    total_c[...] = jnp.zeros_like(total_c)
    total_h[...] = jnp.zeros_like(total_h)

    r, c = iota((4 * CX, CELLS), 0), iota((4 * CX, CELLS), 1)
    target = jnp.where(r < 16, CZ - 2, 0) + (r & 1)
    keep = (((r >> 1) & 7) == (c >> 5)) & ((c & 31) == target)
    pz[...] = jnp.where(keep, 1.0, 0.0).astype(BF16)

    def turn(i, carry):
        part = None
        for j in range(per):
            y = i * per + j
            block = u_v[:, y].reshape(CELLS, NV)
            turned = block.T
            ut[y + 2] = turned
            both = dot_nn(jnp.concatenate([turned, pz[...]], axis=0), block)
            zs[y] = both[NV:].astype(BF16).reshape(2, 2 * CX, NV)
            part = both[:NV] if part is None else part + both[:NV]
        total_c[...] += part
        return carry

    for i in range(LOADS):
        loads[i].wait()
        lax.fori_loop(i, i + 1, turn, 0)

    pl.semaphore_wait(barrier, nx + ny * nz - 2)
    for side in range(2):
        @pl.when(sends("gx", side))
        def _():
            for n in range(PIECES):
                x_early(side, n).start()

        @pl.when(sends("gz", side))
        def _():
            z_copy(side, 0).start()

    slices = ny * nz
    thin = NV // slices

    def total(ref, count):
        parts = [ref[i] for i in range(count)]
        while len(parts) > 1:
            parts = [a + b for a, b in zip(parts[::2], parts[1::2])] + parts[len(parts) & ~1 :]
        return parts[0]

    def post(stage, source, target, peer):
        pltpu.make_async_remote_copy(
            src_ref=source, dst_ref=target, send_sem=ar_send.at[stage], recv_sem=ar_recv.at[stage],
            device_id=peer, device_id_type=MESH,
        ).start()

    def finish(stage, like, count):
        whole = like.at[pl.ds(0, count)]
        pltpu.make_async_copy(whole, whole, ar_recv.at[stage]).wait()
        pltpu.make_async_copy(whole, whole, ar_send.at[stage]).wait()

    def scatter(base, whole, source, part):
        for i in range(slices):
            source[i] = whole[i * thin : (i + 1) * thin, :]
        for there, peer in plane:
            post(base, source.at[there], part.at[here], peer)
        part[here] = source[here]

    def across(base, part, x):
        finish(base, part, slices - 1)
        x[gx] = total(part, slices)
        for peer in rows_of_x:
            post(base + 1, x.at[gx], x.at[gx], peer)

    def gather(base, x, out):
        finish(base + 1, x, nx - 1)
        out[here] = total(x, nx)
        for _, peer in plane:
            post(base + 2, out.at[here], out.at[here], peer)

    def gathered(base, out):
        finish(base + 2, out, slices - 1)
        return jnp.concatenate([out[i] for i in range(slices)], axis=0)

    scatter(0, total_c, c_in, c_part)
    for side in range(2):
        @pl.when(sends("gz", side))
        def _():
            z_copy(side, 1).start()

        @pl.when(sends("gy", side))
        def _():
            y_copy(side).start()

    for side in range(2):
        @pl.when(jnp.logical_not(receives("gx", side)))
        def _():
            def clear(y, carry):
                hx[side, :, y] = jnp.zeros((2, CZ, NV), BF16)
                return carry
            lax.fori_loop(0, CY, clear, 0)

        @pl.when(jnp.logical_not(receives("gy", side)))
        def _():
            hy[side] = jnp.zeros((CX, 2, CZ, NV), BF16)

        @pl.when(jnp.logical_not(receives("gz", side)))
        def _():
            def clear(y, carry):
                hz[y, side] = jnp.zeros((2 * CX, NV), BF16)
                return carry
            lax.fori_loop(0, CY, clear, 0)

    high = ut[2 : HALF + 2, :, NV:].reshape(HALF * NV, NV)
    low = ut[HALF + 2 : CY + 2, :, :NV].reshape(HALF * NV, NV)
    both = dot_nn(jnp.concatenate([high, low], axis=1), bg[...])
    xc[...] = both.astype(BF16).reshape(HALF, NV, NV)

    pot_load.wait()
    pott[...] = potv[...].reshape(CELLS, CY).T * -24.0
    ut[0:2] = jnp.zeros((2, NV, CELLS), BF16)
    ut[CY + 2 : CY + 4] = jnp.zeros((2, NV, CELLS), BF16)

    span = CY // ZPIECES

    def apply(first):
        halo = [hz[first + j].reshape(4 * CX, NV).T for j in range(span)]
        rows = jnp.concatenate(
            [ut[first + 2 : first + 2 + span].reshape(span * NV, CELLS), jnp.concatenate(halo, axis=0)],
            axis=1,
        )
        acc = dot_nn(rows, jnp.concatenate([at[...], ez[...]], axis=0))
        for strip in range(0, NV, 16):
            part = slice(strip, strip + 16)
            cell = [ut[first + j, part, :].astype(F32) for j in range(span + 4)]
            for j in range(span):
                y = first + j
                value = acc[j * NV + strip : j * NV + strip + 16]
                value = value + (16.0 * (cell[j + 1] + cell[j + 3]) - (cell[j] + cell[j + 4]))
                value = value + pott[y : y + 1, :] * cell[j + 2]
                appl[y, part, :] = value
                rounded[y, part, :] = value.astype(BF16)

    def product(cells):
        part = None
        for y in cells:
            term = dot_nt(ut[y + 2], rounded[y])
            part = term if part is None else part + term
        total_h[...] += part

    def z_arrived(i):
        for side in range(2):
            @pl.when(receives("gz", side))
            def _():
                z_copy(side, i).wait_recv()

    z_arrived(0)
    apply(0)
    across(0, c_part, c_x)
    z_arrived(1)
    apply(span)
    product(range(2, span))

    for side in range(2):
        @pl.when(receives("gy", side))
        def _():
            y_copy(side).wait_recv()
    for side, far, near in ((0, 0, 1), (1, CY - 1, CY - 2)):
        first = hy[side, :, 1 - side].reshape(CELLS, NV).T.astype(F32)
        second = hy[side, :, side].reshape(CELLS, NV).T.astype(F32)
        appl[far] += 16.0 * first - second
        appl[near] -= first
        rounded[far] = appl[far].astype(BF16)
        rounded[near] = appl[near].astype(BF16)
    product([0, 1, *range(span, CY)])
    for side in range(2):
        @pl.when(sends("gx", side))
        def _():
            for i in range(LATE - LAST):
                x_late(side, i).start()


    for i in range(PIECES):
        for side in range(2):
            @pl.when(receives("gx", side))
            def _():
                x_early(side, i).wait_recv()
        part = None
        for j in range(early_n):
            p = i * early_n + j
            layers = jnp.concatenate(
                [hx[1, :, p].reshape(2 * CZ, NV), hx[0, :, p + HALF].reshape(2 * CZ, NV)], axis=0
            )
            term = dot_nn(xc[p], layers)
            part = term if part is None else part + term
        total_h[...] += part

    scatter(3, total_h, h_in, h_part)

    gather(0, c_x, c_out)

    def widen(late):
        for i in range(2):
            side = i if late else 1 - i
            halo = [hx[side, :, i * HALF + j].reshape(2 * CZ, NV).T for j in range(HALF)]
            taps = bt[side * 2 * CZ : (side + 1) * 2 * CZ, side * NV : (side + 1) * NV]
            more = dot_nn(jnp.concatenate(halo, axis=0), taps).reshape(HALF, NV, NV)
            appl[i * HALF : (i + 1) * HALF, :, side * NV : (side + 1) * NV] += more

    widen(False)
    across(3, h_part, h_x)

    mat[...] = gathered(0, c_out) * (1.0 / ncell)

    prow, lane = iota((8, NV), 0), iota((8, NV), 1)
    outside = iota((NV, NV), 1) >= 8

    def spread(x, s):
        return jnp.broadcast_to(x[s : s + 1, :], (8, NV))

    def split(x):
        a = x.astype(BF16).astype(F32)
        b = (x - a).astype(BF16).astype(F32)
        return a, b, x - a - b

    def eliminate(b, carry):
        panel = mat[0:8, :]
        column = [jnp.broadcast_to(panel[:, s : s + 1], (8, NV)) for s in range(8)]
        inverse = jnp.zeros((8, NV), F32)
        for s in range(8):
            below = prow > s
            scale = 1.0 / spread(column[s], s)
            factor = jnp.where(below, column[s] * scale, 0.0)
            inverse = jnp.where(prow == s, scale, inverse)
            row = jnp.where(lane == s, 1.0, spread(panel, s))
            panel = jnp.where(below & (lane == s), 0.0, panel) - factor * row
            for t in range(s + 1, 8):
                column[t] = column[t] - factor * spread(column[t], s)
        left = jnp.where((lane >= 8) & (lane < NV - 8 * b), panel, 0.0)
        unit = jnp.where(lane < prow, panel, jnp.where(lane == prow, 1.0, 0.0))
        right = pltpu.roll(jnp.where(lane < 8, unit, panel) * inverse, NV - 8, 1)
        p0, p1, p2 = split(left)
        q0, q1, q2 = split(right)
        left = jnp.concatenate([p0, p0, p1, p0, p1, p2], axis=0).astype(BF16).T
        right = jnp.concatenate([q0, q1, q0, q2, q1, q0], axis=0).astype(BF16)
        rest = pltpu.roll(jnp.where(outside, mat[...], 0.0), NV - 8, 1) - dot_nn(left, right)
        mat[0 : NV - 8, :] = rest[8:, :]
        mat[NV - 8 :, :] = pltpu.roll(panel, NV - 8, 1)
        return carry

    lax.fori_loop(0, 7, eliminate, 0)
    gather(3, h_x, h_out)
    for side in range(2):
        @pl.when(sends("gx", side))
        def _():
            for i in range(LATE - LAST, LATE):
                x_late(side, i).start()
    lax.fori_loop(7, 16, eliminate, 0)

    row_of, lane_of = iota((NV, NV), 0), iota((NV, NV), 1)
    one = jnp.where(row_of == lane_of, 1.0, 0.0)
    done = mat[...]
    diag = jnp.sum(done * one, axis=1, keepdims=True)
    lower = jnp.where(row_of > lane_of, done, one) * lax.rsqrt(diag)
    linv[...] = lower
    linvt[...] = lower.T

    for i in range(LATE):
        for side in range(2):
            @pl.when(receives("gx", side))
            def _():
                x_late(side, i).wait_recv()
    widen(True)

    lower = linv[...]
    hamil = gathered(3, h_out) * (-1.0 / (24.0 * ncell))
    raw = exact_nt(exact(lower, hamil), lower)
    shifted = 0.5 * (raw + raw.T) - one * (jnp.sum(raw * one) / NV)
    scale = lax.rsqrt(jnp.full((1, 1), jnp.sum(shifted * shifted) + 1e-06, F32))
    square = three(shifted, shifted) * (scale * scale)
    sign = shifted * scale
    for step in range(FILTER_STEPS):
        if step > 0:
            square = three(sign, sign)
        sign = 1.5 * sign - 0.5 * three(square, sign)
    rot = exact(linvt[...], exact(0.5 * (one - sign), lower))
    rot = (0.5 * (rot + rot.T)).astype(BF16)

    def densities(i, carry):
        for j in range(STACK):
            y = i * STACK + j
            own = ut[y + 2]
            mixed = dot_nn(rot, own)
            rows_d[pl.ds(y, 1), :] = jnp.sum(own.astype(F32) * mixed, axis=0, keepdims=True)
            rows_e[pl.ds(y, 1), :] = jnp.sum(appl[y] * mixed, axis=0, keepdims=True)
        return carry

    lax.fori_loop(0, CY // STACK, densities, 0)

    for side in range(2):
        @pl.when(sends("gx", side))
        def _():
            for i in range(PIECES):
                x_early(side, i).wait_send()
            for i in range(LATE):
                x_late(side, i).wait_send()

        @pl.when(sends("gy", side))
        def _():
            y_copy(side).wait_send()

        @pl.when(sends("gz", side))
        def _():
            for i in range(ZPIECES):
                z_copy(side, i).wait_send()


def to_cells(rows_d, rows_e, density, energy):
    density[...] = (rows_d[...].T * (1.0 / NB)).reshape(CX, CZ, CY)
    energy[...] = (rows_e[...].T * (-1.0 / (24.0 * NB))).reshape(CX, CZ, CY)


def body(subspace, potential):
    sizes = tuple(lax.axis_size(name) for name in AXES)
    nx, ny, nz = sizes
    vm, dma = pltpu.VMEM, pltpu.SemaphoreType.DMA
    any_space = pl.BlockSpec(memory_space=pltpu.HBM)
    whole = pl.BlockSpec(memory_space=pltpu.VMEM)
    rows_out = jax.ShapeDtypeStruct((CY, CELLS), F32)
    out = jax.ShapeDtypeStruct((CX, CZ, CY), F32)
    slices = ny * nz
    thin = NV // slices
    reduce_set = [
        vm((NV, NV), F32),
        vm((slices, thin, NV), F32), vm((slices, thin, NV), F32),
        vm((nx, thin, NV), F32), vm((slices, thin, NV), F32),
    ]
    rows_d, rows_e = pl.pallas_call(
        functools.partial(kernel, sizes),
        out_shape=(rows_out, rows_out),
        in_specs=[any_space, any_space],
        out_specs=(whole, whole),
        scratch_shapes=[
            vm((CX, CY, CZ, NV), BF16),
            vm((CY + 4, NV, CELLS), BF16),
            vm((CY, NV, CELLS), F32),
            vm((CY, NV, CELLS), BF16),
            vm((2, 2, CY, CZ, NV), BF16),
            vm((2, CX, 2, CZ, NV), BF16),
            vm((CY, 2, 2 * CX, NV), BF16),
            vm((CY, 2, 2 * CX, NV), BF16),
            vm((HALF, NV, NV), BF16),
            vm((CX, CZ, CY), F32),
            vm((CY, CELLS), F32),
            vm((CELLS, CELLS), BF16),
            vm((4 * CX, CELLS), BF16),
            vm((NV, CELLS), BF16),
            vm((CELLS, NV), BF16),
            vm((4 * CX, CELLS), BF16),
            *reduce_set,
            *reduce_set,
            vm((NV, NV), F32),
            vm((NV, NV), F32),
            vm((NV, NV), F32),
            dma((LOADS + 1,)),
            dma((2, PIECES + LATE)),
            dma((2, PIECES + LATE)),
            dma((2,)),
            dma((2,)),
            dma((2, ZPIECES)),
            dma((2, ZPIECES)),
            dma((6,)),
            dma((6,)),
        ],
        compiler_params=pltpu.CompilerParams(
            collective_id=0, has_side_effects=True, vmem_limit_bytes=55072 * 1024
        ),
    )(subspace, jnp.transpose(potential, (0, 2, 1)))
    density, energy = pl.pallas_call(
        to_cells,
        out_shape=(out, out),
        in_specs=[whole, whole],
        out_specs=(whole, whole),
        compiler_params=pltpu.CompilerParams(vmem_limit_bytes=8 * 1024 * 1024),
    )(rows_d, rows_e)
    return jnp.transpose(density, (0, 2, 1)), jnp.transpose(energy, (0, 2, 1))


def solution(mesh):
    return jax.shard_map(
        body,
        mesh=mesh,
        in_specs=(P("gx", "gy", "gz", None), P("gx", "gy", "gz")),
        out_specs=(P("gx", "gy", "gz"), P("gx", "gy", "gz")),
        check_vma=False,
    )
```

```python
import functools

import jax
import jax.numpy as jnp
from jax import lax
from jax.experimental import pallas as pl
from jax.experimental.pallas import tpu as pltpu
from jax.sharding import PartitionSpec as P

NB = 64
FILTER_STEPS = 8
MESH = pl.DeviceIdType.MESH
AXES = ("gx", "gy", "gz")
F32, BF16 = jnp.float32, jnp.bfloat16

CX, CY, CZ, NV = 8, 48, 32, 128
CELLS = CX * CZ
HALF = CY // 2
LOADS = 2
PIECES = 4
LATE = (18, 6)
ZPIECES = 2
STACK = 16


def place(axis, index):
    return tuple(index if name == axis else lax.axis_index(name) for name in AXES)


def iota(shape, dim):
    return lax.broadcasted_iota(jnp.int32, shape, dim)


def tap(distance):
    return jnp.where(distance == 1, 16.0, 0.0) - jnp.where(distance == 2, 1.0, 0.0)


def dot_nn(a, b):
    return jnp.dot(a, b, preferred_element_type=F32)


def dot_nt(a, b):
    return lax.dot_general(a, b, (((1,), (1,)), ((), ())), preferred_element_type=F32)


def exact(a, b):
    return jnp.dot(a, b, precision=lax.Precision.HIGHEST, preferred_element_type=F32)


def three(a, b):
    a0, b0 = a.astype(BF16), b.astype(BF16)
    a1, b1 = (a - a0.astype(F32)).astype(BF16), (b - b0.astype(F32)).astype(BF16)
    return dot_nn(jnp.concatenate([a0, a0, a1], axis=1), jnp.concatenate([b0, b1, b0], axis=0))


def exact_nt(a, b):
    return lax.dot_general(
        a, b, (((1,), (1,)), ((), ())), precision=lax.Precision.HIGHEST, preferred_element_type=F32
    )


def kernel(
    sizes, u_hbm, pot_hbm, rows_d, rows_e,
    u_v, ut, appl, rounded, hx, hy, hz, zs, xc, potv, pott, at, ez, bt, bg, pz,
    total_c, c_in, c_part, c_x, c_out, total_h, h_in, h_part, h_x, h_out, mat, linv, linvt,
    load_sem, x_send, x_recv, y_send, y_recv, z_send, z_recv, ar_send, ar_recv,
):
    size = dict(zip(AXES, sizes))
    me = {name: lax.axis_index(name) for name in AXES}
    gx, gy, gz = me["gx"], me["gy"], me["gz"]
    nx, ny, nz = sizes
    ncell = float(nx * ny * nz * CX * CY * CZ)

    per = CY // LOADS
    loads = []
    for i in range(LOADS):
        span = pl.ds(i * per, per)
        loads.append(pltpu.make_async_copy(u_hbm.at[:, span], u_v.at[:, span], load_sem.at[i]))
        loads[-1].start()
    pot_load = pltpu.make_async_copy(pot_hbm, potv, load_sem.at[LOADS])
    pot_load.start()

    barrier = pltpu.get_barrier_semaphore()
    rows_of_x = [place("gx", lax.rem(gx + off, nx)) for off in range(1, nx)]
    plane = []
    for off in range(1, ny * nz):
        py, pz_at = lax.rem(gy + off // nz, ny), lax.rem(gz + off % nz, nz)
        plane.append((py * nz + pz_at, (gx, py, pz_at)))
    here = gy * nz + gz
    for peer in rows_of_x + [peer for _, peer in plane]:
        pl.semaphore_signal(barrier, inc=1, device_id=peer, device_id_type=MESH)

    def send(src, dst, ssem, rsem, axis, peer):
        return pltpu.make_async_remote_copy(
            src_ref=src, dst_ref=dst, send_sem=ssem, recv_sem=rsem,
            device_id=place(axis, peer), device_id_type=MESH,
        )

    def x_copy(side, start, count, slot):
        layers = pl.ds(CX - 2, 2) if side == 0 else pl.ds(0, 2)
        span = pl.ds(start, count)
        peer = lax.rem(gx + 1, nx) if side == 0 else lax.rem(gx + nx - 1, nx)
        return send(
            u_hbm.at[layers, span], hx.at[side, :, span],
            x_send.at[side], x_recv.at[side, slot], "gx", peer,
        )

    early_n = HALF // PIECES

    def x_early(side, i):
        return x_copy(side, (HALF if side == 0 else 0) + i * early_n, early_n, i)

    def x_late(side, i):
        return x_copy(side, (0 if side == 0 else HALF) + sum(LATE[:i]), LATE[i], PIECES + i)

    def y_copy(side):
        layers = pl.ds(CY - 2, 2) if side == 0 else pl.ds(0, 2)
        peer = lax.rem(gy + 1, ny) if side == 0 else lax.rem(gy + ny - 1, ny)
        return send(
            u_hbm.at[:, layers], hy.at[side], y_send.at[side], y_recv.at[side], "gy", peer
        )

    def z_copy(side, i):
        span = pl.ds(i * (CY // ZPIECES), CY // ZPIECES)
        peer = lax.rem(gz + 1, nz) if side == 0 else lax.rem(gz + nz - 1, nz)
        return send(
            zs.at[span, side], hz.at[span, side],
            z_send.at[side], z_recv.at[side, i], "gz", peer,
        )

    def sends(axis, side):
        return me[axis] < size[axis] - 1 if side == 0 else me[axis] > 0

    def receives(axis, side):
        return me[axis] > 0 if side == 0 else me[axis] < size[axis] - 1

    r, c = iota((CELLS, CELLS), 0), iota((CELLS, CELLS), 1)
    same_x, same_z = (r >> 5) == (c >> 5), (r & 31) == (c & 31)
    along_z = jnp.where(same_x, tap(jnp.abs((r & 31) - (c & 31))), 0.0)
    along_x = jnp.where(same_z, tap(jnp.abs((r >> 5) - (c >> 5))), 0.0)
    at[...] = (along_x + along_z - jnp.where(r == c, 90.0, 0.0)).astype(BF16)

    r, c = iota((NV, CELLS), 0), iota((NV, CELLS), 1)
    k, x = (r >> 5) & 1, c >> 5
    dist = jnp.where(r < 64, x + 2 - k, CX + k - x)
    bt[...] = jnp.where((r & 31) == (c & 31), tap(dist), 0.0).astype(BF16)

    r, c = iota((CELLS, NV), 0), iota((CELLS, NV), 1)
    k, x = (c >> 5) & 1, (r >> 5) & 3
    dist = jnp.where(c < 64, CX // 2 + k - x, x + 2 - k)
    keep = ((r & 31) == (c & 31)) & ((r < NV) == (c < 64))
    bg[...] = jnp.where(keep, 2.0 * tap(dist), 0.0).astype(BF16)

    r, c = iota((4 * CX, CELLS), 0), iota((4 * CX, CELLS), 1)
    k, z = r & 1, c & 31
    dist = jnp.where(r < 16, z + 2 - k, CZ + k - z)
    ez[...] = jnp.where(((r >> 1) & 7) == (c >> 5), tap(dist), 0.0).astype(BF16)

    total_c[...] = jnp.zeros_like(total_c)
    total_h[...] = jnp.zeros_like(total_h)

    r, c = iota((4 * CX, CELLS), 0), iota((4 * CX, CELLS), 1)
    target = jnp.where(r < 16, CZ - 2, 0) + (r & 1)
    keep = (((r >> 1) & 7) == (c >> 5)) & ((c & 31) == target)
    pz[...] = jnp.where(keep, 1.0, 0.0).astype(BF16)

    def turn(i, carry):
        part = None
        for j in range(per):
            y = i * per + j
            block = u_v[:, y].reshape(CELLS, NV)
            turned = block.T
            ut[y + 2] = turned
            both = dot_nn(jnp.concatenate([turned, pz[...]], axis=0), block)
            zs[y] = both[NV:].astype(BF16).reshape(2, 2 * CX, NV)
            part = both[:NV] if part is None else part + both[:NV]
        total_c[...] += part
        return carry

    for i in range(LOADS):
        loads[i].wait()
        lax.fori_loop(i, i + 1, turn, 0)

    pl.semaphore_wait(barrier, nx + ny * nz - 2)
    for side in range(2):
        @pl.when(sends("gx", side))
        def _():
            for n in range(PIECES):
                x_early(side, n).start()

        @pl.when(sends("gz", side))
        def _():
            z_copy(side, 0).start()

    slices = ny * nz
    thin = NV // slices

    def total(ref, count):
        parts = [ref[i] for i in range(count)]
        while len(parts) > 1:
            parts = [a + b for a, b in zip(parts[::2], parts[1::2])] + parts[len(parts) & ~1 :]
        return parts[0]

    def post(stage, source, target, peer):
        pltpu.make_async_remote_copy(
            src_ref=source, dst_ref=target, send_sem=ar_send.at[stage // 3], recv_sem=ar_recv.at[stage],
            device_id=peer, device_id_type=MESH,
        ).start()

    def finish(stage, like, count):
        whole = like.at[pl.ds(0, count)]
        pltpu.make_async_copy(whole, whole, ar_recv.at[stage]).wait()
        pltpu.make_async_copy(whole, whole, ar_send.at[stage // 3]).wait()

    def scatter(base, whole, source, part):
        for i in range(slices):
            source[i] = whole[i * thin : (i + 1) * thin, :]
        for there, peer in plane:
            post(base, source.at[there], part.at[here], peer)
        part[here] = source[here]

    def across(base, part, x):
        finish(base, part, slices - 1)
        x[gx] = total(part, slices)
        for peer in rows_of_x:
            post(base + 1, x.at[gx], x.at[gx], peer)

    def gather(base, x, out):
        finish(base + 1, x, nx - 1)
        out[here] = total(x, nx)
        for _, peer in plane:
            post(base + 2, out.at[here], out.at[here], peer)

    def gathered(base, out):
        finish(base + 2, out, slices - 1)
        return jnp.concatenate([out[i] for i in range(slices)], axis=0)

    scatter(0, total_c, c_in, c_part)
    for side in range(2):
        @pl.when(sends("gz", side))
        def _():
            z_copy(side, 1).start()

        @pl.when(sends("gy", side))
        def _():
            y_copy(side).start()

    for side in range(2):
        @pl.when(jnp.logical_not(receives("gx", side)))
        def _():
            def clear(y, carry):
                hx[side, :, y] = jnp.zeros((2, CZ, NV), BF16)
                return carry
            lax.fori_loop(0, CY, clear, 0)

        @pl.when(jnp.logical_not(receives("gy", side)))
        def _():
            hy[side] = jnp.zeros((CX, 2, CZ, NV), BF16)

        @pl.when(jnp.logical_not(receives("gz", side)))
        def _():
            def clear(y, carry):
                hz[y, side] = jnp.zeros((2 * CX, NV), BF16)
                return carry
            lax.fori_loop(0, CY, clear, 0)

    high = ut[2 : HALF + 2, :, NV:].reshape(HALF * NV, NV)
    low = ut[HALF + 2 : CY + 2, :, :NV].reshape(HALF * NV, NV)
    both = dot_nn(jnp.concatenate([high, low], axis=1), bg[...])
    xc[...] = both.astype(BF16).reshape(HALF, NV, NV)

    pot_load.wait()
    pott[...] = potv[...].reshape(CELLS, CY).T * -24.0
    ut[0:2] = jnp.zeros((2, NV, CELLS), BF16)
    ut[CY + 2 : CY + 4] = jnp.zeros((2, NV, CELLS), BF16)

    span = CY // ZPIECES

    def apply(first):
        halo = [hz[first + j].reshape(4 * CX, NV).T for j in range(span)]
        rows = jnp.concatenate(
            [ut[first + 2 : first + 2 + span].reshape(span * NV, CELLS), jnp.concatenate(halo, axis=0)],
            axis=1,
        )
        acc = dot_nn(rows, jnp.concatenate([at[...], ez[...]], axis=0))
        for strip in range(0, NV, 16):
            part = slice(strip, strip + 16)
            cell = [ut[first + j, part, :].astype(F32) for j in range(span + 4)]
            for j in range(span):
                y = first + j
                value = acc[j * NV + strip : j * NV + strip + 16]
                value = value + (16.0 * (cell[j + 1] + cell[j + 3]) - (cell[j] + cell[j + 4]))
                value = value + pott[y : y + 1, :] * cell[j + 2]
                appl[y, part, :] = value
                rounded[y, part, :] = value.astype(BF16)

    def product(cells):
        part = None
        for y in cells:
            term = dot_nt(ut[y + 2], rounded[y])
            part = term if part is None else part + term
        total_h[...] += part

    def z_arrived(i):
        for side in range(2):
            @pl.when(receives("gz", side))
            def _():
                z_copy(side, i).wait_recv()

    z_arrived(0)
    apply(0)
    across(0, c_part, c_x)
    z_arrived(1)
    apply(span)
    product(range(2, span))

    for side in range(2):
        @pl.when(receives("gy", side))
        def _():
            y_copy(side).wait_recv()
    for side, far, near in ((0, 0, 1), (1, CY - 1, CY - 2)):
        first = hy[side, :, 1 - side].reshape(CELLS, NV).T.astype(F32)
        second = hy[side, :, side].reshape(CELLS, NV).T.astype(F32)
        appl[far] += 16.0 * first - second
        appl[near] -= first
        rounded[far] = appl[far].astype(BF16)
        rounded[near] = appl[near].astype(BF16)
    product([0, 1, *range(span, CY)])
    for side in range(2):
        @pl.when(sends("gx", side))
        def _():
            x_late(side, 0).start()


    for i in range(PIECES):
        for side in range(2):
            @pl.when(receives("gx", side))
            def _():
                x_early(side, i).wait_recv()
        part = None
        for j in range(early_n):
            p = i * early_n + j
            layers = jnp.concatenate(
                [hx[1, :, p].reshape(2 * CZ, NV), hx[0, :, p + HALF].reshape(2 * CZ, NV)], axis=0
            )
            term = dot_nn(xc[p], layers)
            part = term if part is None else part + term
        total_h[...] += part

    scatter(3, total_h, h_in, h_part)

    gather(0, c_x, c_out)

    def widen(late):
        for i in range(2):
            side = i if late else 1 - i
            halo = [hx[side, :, i * HALF + j].reshape(2 * CZ, NV).T for j in range(HALF)]
            taps = bt[side * 2 * CZ : (side + 1) * 2 * CZ, side * NV : (side + 1) * NV]
            more = dot_nn(jnp.concatenate(halo, axis=0), taps).reshape(HALF, NV, NV)
            appl[i * HALF : (i + 1) * HALF, :, side * NV : (side + 1) * NV] += more

    widen(False)
    across(3, h_part, h_x)

    mat[...] = gathered(0, c_out) * (1.0 / ncell)

    prow, lane = iota((8, NV), 0), iota((8, NV), 1)
    outside = iota((NV, NV), 1) >= 8

    def spread(x, s):
        return jnp.broadcast_to(x[s : s + 1, :], (8, NV))

    def split(x):
        a = x.astype(BF16).astype(F32)
        b = (x - a).astype(BF16).astype(F32)
        return a, b, x - a - b

    def eliminate(b, carry):
        panel = mat[0:8, :]
        column = [jnp.broadcast_to(panel[:, s : s + 1], (8, NV)) for s in range(8)]
        inverse = jnp.zeros((8, NV), F32)
        for s in range(8):
            below = prow > s
            scale = 1.0 / spread(column[s], s)
            factor = jnp.where(below, column[s] * scale, 0.0)
            inverse = jnp.where(prow == s, scale, inverse)
            row = jnp.where(lane == s, 1.0, spread(panel, s))
            panel = jnp.where(below & (lane == s), 0.0, panel) - factor * row
            for t in range(s + 1, 8):
                column[t] = column[t] - factor * spread(column[t], s)
        left = jnp.where((lane >= 8) & (lane < NV - 8 * b), panel, 0.0)
        unit = jnp.where(lane < prow, panel, jnp.where(lane == prow, 1.0, 0.0))
        right = pltpu.roll(jnp.where(lane < 8, unit, panel) * inverse, NV - 8, 1)
        p0, p1, p2 = split(left)
        q0, q1, q2 = split(right)
        left = jnp.concatenate([p0, p0, p1, p0, p1, p2], axis=0).astype(BF16).T
        right = jnp.concatenate([q0, q1, q0, q2, q1, q0], axis=0).astype(BF16)
        rest = pltpu.roll(jnp.where(outside, mat[...], 0.0), NV - 8, 1) - dot_nn(left, right)
        mat[0 : NV - 8, :] = rest[8:, :]
        mat[NV - 8 :, :] = pltpu.roll(panel, NV - 8, 1)
        return carry

    lax.fori_loop(0, 7, eliminate, 0)
    gather(3, h_x, h_out)
    for side in range(2):
        @pl.when(sends("gx", side))
        def _():
            x_late(side, 1).start()
    lax.fori_loop(7, 16, eliminate, 0)

    row_of, lane_of = iota((NV, NV), 0), iota((NV, NV), 1)
    one = jnp.where(row_of == lane_of, 1.0, 0.0)
    done = mat[...]
    diag = jnp.sum(done * one, axis=1, keepdims=True)
    lower = jnp.where(row_of > lane_of, done, one) * lax.rsqrt(diag)
    linv[...] = lower
    linvt[...] = lower.T

    for i in range(len(LATE)):
        for side in range(2):
            @pl.when(receives("gx", side))
            def _():
                x_late(side, i).wait_recv()
    widen(True)

    lower = linv[...]
    hamil = gathered(3, h_out) * (-1.0 / (24.0 * ncell))
    raw = exact_nt(exact(lower, hamil), lower)
    shifted = 0.5 * (raw + raw.T) - one * (jnp.sum(raw * one) / NV)
    scale = lax.rsqrt(jnp.full((1, 1), jnp.sum(shifted * shifted) + 1e-06, F32))
    square = three(shifted, shifted) * (scale * scale)
    sign = shifted * scale
    for step in range(FILTER_STEPS):
        if step > 0:
            square = three(sign, sign)
        sign = 1.5 * sign - 0.5 * three(square, sign)
    rot = exact(linvt[...], exact(0.5 * (one - sign), lower))
    rot = (0.5 * (rot + rot.T)).astype(BF16)

    def densities(i, carry):
        for j in range(STACK):
            y = i * STACK + j
            own = ut[y + 2]
            mixed = dot_nn(rot, own)
            rows_d[pl.ds(y, 1), :] = jnp.sum(own.astype(F32) * mixed, axis=0, keepdims=True)
            rows_e[pl.ds(y, 1), :] = jnp.sum(appl[y] * mixed, axis=0, keepdims=True)
        return carry

    lax.fori_loop(0, CY // STACK, densities, 0)

    for side in range(2):
        @pl.when(sends("gx", side))
        def _():
            x_copy(side, 0, CY, 0).wait_send()

        @pl.when(sends("gy", side))
        def _():
            y_copy(side).wait_send()

        @pl.when(sends("gz", side))
        def _():
            whole = zs.at[:, side]
            pltpu.make_async_copy(whole, whole, z_send.at[side]).wait()


def to_cells(rows_d, rows_e, density, energy):
    density[...] = (rows_d[...].T * (1.0 / NB)).reshape(CX, CZ, CY)
    energy[...] = (rows_e[...].T * (-1.0 / (24.0 * NB))).reshape(CX, CZ, CY)


def body(subspace, potential):
    sizes = tuple(lax.axis_size(name) for name in AXES)
    nx, ny, nz = sizes
    vm, dma = pltpu.VMEM, pltpu.SemaphoreType.DMA
    any_space = pl.BlockSpec(memory_space=pltpu.HBM)
    whole = pl.BlockSpec(memory_space=pltpu.VMEM)
    rows_out = jax.ShapeDtypeStruct((CY, CELLS), F32)
    out = jax.ShapeDtypeStruct((CX, CZ, CY), F32)
    slices = ny * nz
    thin = NV // slices
    reduce_set = [
        vm((NV, NV), F32),
        vm((slices, thin, NV), F32), vm((slices, thin, NV), F32),
        vm((nx, thin, NV), F32), vm((slices, thin, NV), F32),
    ]
    rows_d, rows_e = pl.pallas_call(
        functools.partial(kernel, sizes),
        out_shape=(rows_out, rows_out),
        in_specs=[any_space, any_space],
        out_specs=(whole, whole),
        scratch_shapes=[
            vm((CX, CY, CZ, NV), BF16),
            vm((CY + 4, NV, CELLS), BF16),
            vm((CY, NV, CELLS), F32),
            vm((CY, NV, CELLS), BF16),
            vm((2, 2, CY, CZ, NV), BF16),
            vm((2, CX, 2, CZ, NV), BF16),
            vm((CY, 2, 2 * CX, NV), BF16),
            vm((CY, 2, 2 * CX, NV), BF16),
            vm((HALF, NV, NV), BF16),
            vm((CX, CZ, CY), F32),
            vm((CY, CELLS), F32),
            vm((CELLS, CELLS), BF16),
            vm((4 * CX, CELLS), BF16),
            vm((NV, CELLS), BF16),
            vm((CELLS, NV), BF16),
            vm((4 * CX, CELLS), BF16),
            *reduce_set,
            *reduce_set,
            vm((NV, NV), F32),
            vm((NV, NV), F32),
            vm((NV, NV), F32),
            dma((LOADS + 1,)),
            dma((2,)),
            dma((2, PIECES + len(LATE))),
            dma((2,)),
            dma((2,)),
            dma((2,)),
            dma((2, ZPIECES)),
            dma((2,)),
            dma((6,)),
        ],
        compiler_params=pltpu.CompilerParams(
            collective_id=0, has_side_effects=True, vmem_limit_bytes=55072 * 1024
        ),
    )(subspace, jnp.transpose(potential, (0, 2, 1)))
    density, energy = pl.pallas_call(
        to_cells,
        out_shape=(out, out),
        in_specs=[whole, whole],
        out_specs=(whole, whole),
        compiler_params=pltpu.CompilerParams(vmem_limit_bytes=8 * 1024 * 1024),
    )(rows_d, rows_e)
    return jnp.transpose(density, (0, 2, 1)), jnp.transpose(energy, (0, 2, 1))


def solution(mesh):
    return jax.shard_map(
        body,
        mesh=mesh,
        in_specs=(P("gx", "gy", "gz", None), P("gx", "gy", "gz")),
        out_specs=(P("gx", "gy", "gz"), P("gx", "gy", "gz")),
        check_vma=False,
    )
```

```python
import functools

import jax
import jax.numpy as jnp
from jax import lax
from jax.experimental import pallas as pl
from jax.experimental.pallas import tpu as pltpu
from jax.sharding import PartitionSpec as P

NB = 64
FILTER_STEPS = 8
MESH = pl.DeviceIdType.MESH
AXES = ("gx", "gy", "gz")
F32, BF16 = jnp.float32, jnp.bfloat16

CX, CY, CZ, NV = 8, 48, 32, 128
CELLS = CX * CZ
HALF = CY // 2
LOADS = 2
PIECES = 4
LATE = (20, 4)
ZPIECES = 2
STACK = 16


def place(axis, index):
    return tuple(index if name == axis else lax.axis_index(name) for name in AXES)


def iota(shape, dim):
    return lax.broadcasted_iota(jnp.int32, shape, dim)


def tap(distance):
    return jnp.where(distance == 1, 16.0, 0.0) - jnp.where(distance == 2, 1.0, 0.0)


def dot_nn(a, b):
    return jnp.dot(a, b, preferred_element_type=F32)


def dot_nt(a, b):
    return lax.dot_general(a, b, (((1,), (1,)), ((), ())), preferred_element_type=F32)


def exact(a, b):
    return jnp.dot(a, b, precision=lax.Precision.HIGHEST, preferred_element_type=F32)


def three(a, b):
    a0, b0 = a.astype(BF16), b.astype(BF16)
    a1, b1 = (a - a0.astype(F32)).astype(BF16), (b - b0.astype(F32)).astype(BF16)
    return dot_nn(jnp.concatenate([a0, a0, a1], axis=1), jnp.concatenate([b0, b1, b0], axis=0))


def exact_nt(a, b):
    return lax.dot_general(
        a, b, (((1,), (1,)), ((), ())), precision=lax.Precision.HIGHEST, preferred_element_type=F32
    )


def kernel(
    sizes, u_hbm, pot_hbm, rows_d, rows_e,
    u_v, ut, appl, rounded, hx, hy, hz, zs, xc, potv, pott, at, ez, bt, bg, pz,
    total_c, c_in, c_part, c_x, c_out, total_h, h_in, h_part, h_x, h_out, mat, linv, linvt,
    load_sem, x_send, x_recv, y_send, y_recv, z_send, z_recv, ar_send, ar_recv,
):
    size = dict(zip(AXES, sizes))
    me = {name: lax.axis_index(name) for name in AXES}
    gx, gy, gz = me["gx"], me["gy"], me["gz"]
    nx, ny, nz = sizes
    ncell = float(nx * ny * nz * CX * CY * CZ)

    per = CY // LOADS
    loads = []
    for i in range(LOADS):
        span = pl.ds(i * per, per)
        loads.append(pltpu.make_async_copy(u_hbm.at[:, span], u_v.at[:, span], load_sem.at[i]))
        loads[-1].start()
    pot_load = pltpu.make_async_copy(pot_hbm, potv, load_sem.at[LOADS])
    pot_load.start()

    barrier = pltpu.get_barrier_semaphore()
    rows_of_x = [place("gx", lax.rem(gx + off, nx)) for off in range(1, nx)]
    plane = []
    for off in range(1, ny * nz):
        py, pz_at = lax.rem(gy + off // nz, ny), lax.rem(gz + off % nz, nz)
        plane.append((py * nz + pz_at, (gx, py, pz_at)))
    here = gy * nz + gz
    for peer in rows_of_x + [peer for _, peer in plane]:
        pl.semaphore_signal(barrier, inc=1, device_id=peer, device_id_type=MESH)

    def send(src, dst, ssem, rsem, axis, peer):
        return pltpu.make_async_remote_copy(
            src_ref=src, dst_ref=dst, send_sem=ssem, recv_sem=rsem,
            device_id=place(axis, peer), device_id_type=MESH,
        )

    def x_copy(side, start, count, slot):
        layers = pl.ds(CX - 2, 2) if side == 0 else pl.ds(0, 2)
        span = pl.ds(start, count)
        peer = lax.rem(gx + 1, nx) if side == 0 else lax.rem(gx + nx - 1, nx)
        return send(
            u_hbm.at[layers, span], hx.at[side, :, span],
            x_send.at[side], x_recv.at[side, slot], "gx", peer,
        )

    early_n = HALF // PIECES

    def x_early(side, i):
        return x_copy(side, (HALF if side == 0 else 0) + i * early_n, early_n, i)

    def x_late(side, i):
        return x_copy(side, (0 if side == 0 else HALF) + sum(LATE[:i]), LATE[i], PIECES + i)

    def y_copy(side):
        layers = pl.ds(CY - 2, 2) if side == 0 else pl.ds(0, 2)
        peer = lax.rem(gy + 1, ny) if side == 0 else lax.rem(gy + ny - 1, ny)
        return send(
            u_hbm.at[:, layers], hy.at[side], y_send.at[side], y_recv.at[side], "gy", peer
        )

    def z_copy(side, i):
        span = pl.ds(i * (CY // ZPIECES), CY // ZPIECES)
        peer = lax.rem(gz + 1, nz) if side == 0 else lax.rem(gz + nz - 1, nz)
        return send(
            zs.at[span, side], hz.at[span, side],
            z_send.at[side], z_recv.at[side, i], "gz", peer,
        )

    def sends(axis, side):
        return me[axis] < size[axis] - 1 if side == 0 else me[axis] > 0

    def receives(axis, side):
        return me[axis] > 0 if side == 0 else me[axis] < size[axis] - 1

    r, c = iota((CELLS, CELLS), 0), iota((CELLS, CELLS), 1)
    same_x, same_z = (r >> 5) == (c >> 5), (r & 31) == (c & 31)
    along_z = jnp.where(same_x, tap(jnp.abs((r & 31) - (c & 31))), 0.0)
    along_x = jnp.where(same_z, tap(jnp.abs((r >> 5) - (c >> 5))), 0.0)
    at[...] = (along_x + along_z - jnp.where(r == c, 90.0, 0.0)).astype(BF16)

    r, c = iota((NV, CELLS), 0), iota((NV, CELLS), 1)
    k, x = (r >> 5) & 1, c >> 5
    dist = jnp.where(r < 64, x + 2 - k, CX + k - x)
    bt[...] = jnp.where((r & 31) == (c & 31), tap(dist), 0.0).astype(BF16)

    r, c = iota((CELLS, NV), 0), iota((CELLS, NV), 1)
    k, x = (c >> 5) & 1, (r >> 5) & 3
    dist = jnp.where(c < 64, CX // 2 + k - x, x + 2 - k)
    keep = ((r & 31) == (c & 31)) & ((r < NV) == (c < 64))
    bg[...] = jnp.where(keep, 2.0 * tap(dist), 0.0).astype(BF16)

    r, c = iota((4 * CX, CELLS), 0), iota((4 * CX, CELLS), 1)
    k, z = r & 1, c & 31
    dist = jnp.where(r < 16, z + 2 - k, CZ + k - z)
    ez[...] = jnp.where(((r >> 1) & 7) == (c >> 5), tap(dist), 0.0).astype(BF16)

    total_c[...] = jnp.zeros_like(total_c)
    total_h[...] = jnp.zeros_like(total_h)

    r, c = iota((4 * CX, CELLS), 0), iota((4 * CX, CELLS), 1)
    target = jnp.where(r < 16, CZ - 2, 0) + (r & 1)
    keep = (((r >> 1) & 7) == (c >> 5)) & ((c & 31) == target)
    pz[...] = jnp.where(keep, 1.0, 0.0).astype(BF16)

    def turn(i, carry):
        part = None
        for j in range(per):
            y = i * per + j
            block = u_v[:, y].reshape(CELLS, NV)
            turned = block.T
            ut[y + 2] = turned
            both = dot_nn(jnp.concatenate([turned, pz[...]], axis=0), block)
            zs[y] = both[NV:].astype(BF16).reshape(2, 2 * CX, NV)
            part = both[:NV] if part is None else part + both[:NV]
        total_c[...] += part
        return carry

    for i in range(LOADS):
        loads[i].wait()
        lax.fori_loop(i, i + 1, turn, 0)

    pl.semaphore_wait(barrier, nx + ny * nz - 2)
    for side in range(2):
        @pl.when(sends("gx", side))
        def _():
            for n in range(PIECES):
                x_early(side, n).start()

        @pl.when(sends("gz", side))
        def _():
            z_copy(side, 0).start()

    slices = ny * nz
    thin = NV // slices

    def total(ref, count):
        parts = [ref[i] for i in range(count)]
        while len(parts) > 1:
            parts = [a + b for a, b in zip(parts[::2], parts[1::2])] + parts[len(parts) & ~1 :]
        return parts[0]

    def post(stage, source, target, peer):
        pltpu.make_async_remote_copy(
            src_ref=source, dst_ref=target, send_sem=ar_send.at[stage // 3], recv_sem=ar_recv.at[stage],
            device_id=peer, device_id_type=MESH,
        ).start()

    def finish(stage, like, count):
        whole = like.at[pl.ds(0, count)]
        pltpu.make_async_copy(whole, whole, ar_recv.at[stage]).wait()
        pltpu.make_async_copy(whole, whole, ar_send.at[stage // 3]).wait()

    def scatter(base, whole, source, part):
        for i in range(slices):
            source[i] = whole[i * thin : (i + 1) * thin, :]
        for there, peer in plane:
            post(base, source.at[there], part.at[here], peer)
        part[here] = source[here]

    def across(base, part, x):
        finish(base, part, slices - 1)
        x[gx] = total(part, slices)
        for peer in rows_of_x:
            post(base + 1, x.at[gx], x.at[gx], peer)

    def gather(base, x, out):
        finish(base + 1, x, nx - 1)
        out[here] = total(x, nx)
        for _, peer in plane:
            post(base + 2, out.at[here], out.at[here], peer)

    def gathered(base, out):
        finish(base + 2, out, slices - 1)
        return jnp.concatenate([out[i] for i in range(slices)], axis=0)

    scatter(0, total_c, c_in, c_part)
    for side in range(2):
        @pl.when(sends("gz", side))
        def _():
            z_copy(side, 1).start()

        @pl.when(sends("gy", side))
        def _():
            y_copy(side).start()

    for side in range(2):
        @pl.when(jnp.logical_not(receives("gx", side)))
        def _():
            def clear(y, carry):
                hx[side, :, y] = jnp.zeros((2, CZ, NV), BF16)
                return carry
            lax.fori_loop(0, CY, clear, 0)

        @pl.when(jnp.logical_not(receives("gy", side)))
        def _():
            hy[side] = jnp.zeros((CX, 2, CZ, NV), BF16)

        @pl.when(jnp.logical_not(receives("gz", side)))
        def _():
            def clear(y, carry):
                hz[y, side] = jnp.zeros((2 * CX, NV), BF16)
                return carry
            lax.fori_loop(0, CY, clear, 0)

    high = ut[2 : HALF + 2, :, NV:].reshape(HALF * NV, NV)
    low = ut[HALF + 2 : CY + 2, :, :NV].reshape(HALF * NV, NV)
    both = dot_nn(jnp.concatenate([high, low], axis=1), bg[...])
    xc[...] = both.astype(BF16).reshape(HALF, NV, NV)

    pot_load.wait()
    pott[...] = potv[...].reshape(CELLS, CY).T * -24.0
    ut[0:2] = jnp.zeros((2, NV, CELLS), BF16)
    ut[CY + 2 : CY + 4] = jnp.zeros((2, NV, CELLS), BF16)

    span = CY // ZPIECES

    def apply(first):
        halo = [hz[first + j].reshape(4 * CX, NV).T for j in range(span)]
        rows = jnp.concatenate(
            [ut[first + 2 : first + 2 + span].reshape(span * NV, CELLS), jnp.concatenate(halo, axis=0)],
            axis=1,
        )
        acc = dot_nn(rows, jnp.concatenate([at[...], ez[...]], axis=0))
        for strip in range(0, NV, 16):
            part = slice(strip, strip + 16)
            cell = [ut[first + j, part, :].astype(F32) for j in range(span + 4)]
            for j in range(span):
                y = first + j
                value = acc[j * NV + strip : j * NV + strip + 16]
                value = value + (16.0 * (cell[j + 1] + cell[j + 3]) - (cell[j] + cell[j + 4]))
                value = value + pott[y : y + 1, :] * cell[j + 2]
                appl[y, part, :] = value
                rounded[y, part, :] = value.astype(BF16)

    def product(cells):
        part = None
        for y in cells:
            term = dot_nt(ut[y + 2], rounded[y])
            part = term if part is None else part + term
        total_h[...] += part

    def z_arrived(i):
        for side in range(2):
            @pl.when(receives("gz", side))
            def _():
                z_copy(side, i).wait_recv()

    z_arrived(0)
    apply(0)
    across(0, c_part, c_x)
    z_arrived(1)
    apply(span)
    product(range(2, span))

    for side in range(2):
        @pl.when(receives("gy", side))
        def _():
            y_copy(side).wait_recv()
    for side, far, near in ((0, 0, 1), (1, CY - 1, CY - 2)):
        first = hy[side, :, 1 - side].reshape(CELLS, NV).T.astype(F32)
        second = hy[side, :, side].reshape(CELLS, NV).T.astype(F32)
        appl[far] += 16.0 * first - second
        appl[near] -= first
        rounded[far] = appl[far].astype(BF16)
        rounded[near] = appl[near].astype(BF16)
    product([0, 1, *range(span, CY)])
    for side in range(2):
        @pl.when(sends("gx", side))
        def _():
            x_late(side, 0).start()


    for i in range(PIECES):
        for side in range(2):
            @pl.when(receives("gx", side))
            def _():
                x_early(side, i).wait_recv()
        part = None
        for j in range(early_n):
            p = i * early_n + j
            layers = jnp.concatenate(
                [hx[1, :, p].reshape(2 * CZ, NV), hx[0, :, p + HALF].reshape(2 * CZ, NV)], axis=0
            )
            term = dot_nn(xc[p], layers)
            part = term if part is None else part + term
        total_h[...] += part

    scatter(3, total_h, h_in, h_part)

    gather(0, c_x, c_out)

    def widen(late):
        for i in range(2):
            side = i if late else 1 - i
            halo = [hx[side, :, i * HALF + j].reshape(2 * CZ, NV).T for j in range(HALF)]
            taps = bt[side * 2 * CZ : (side + 1) * 2 * CZ, side * NV : (side + 1) * NV]
            more = dot_nn(jnp.concatenate(halo, axis=0), taps).reshape(HALF, NV, NV)
            appl[i * HALF : (i + 1) * HALF, :, side * NV : (side + 1) * NV] += more

    widen(False)
    across(3, h_part, h_x)

    mat[...] = gathered(0, c_out) * (1.0 / ncell)

    prow, lane = iota((8, NV), 0), iota((8, NV), 1)
    outside = iota((NV, NV), 1) >= 8

    def spread(x, s):
        return jnp.broadcast_to(x[s : s + 1, :], (8, NV))

    def split(x):
        a = x.astype(BF16).astype(F32)
        b = (x - a).astype(BF16).astype(F32)
        return a, b, x - a - b

    def eliminate(b, carry):
        panel = mat[0:8, :]
        column = [jnp.broadcast_to(panel[:, s : s + 1], (8, NV)) for s in range(8)]
        inverse = jnp.zeros((8, NV), F32)
        for s in range(8):
            below = prow > s
            scale = 1.0 / spread(column[s], s)
            factor = jnp.where(below, column[s] * scale, 0.0)
            inverse = jnp.where(prow == s, scale, inverse)
            row = jnp.where(lane == s, 1.0, spread(panel, s))
            panel = jnp.where(below & (lane == s), 0.0, panel) - factor * row
            for t in range(s + 1, 8):
                column[t] = column[t] - factor * spread(column[t], s)
        left = jnp.where((lane >= 8) & (lane < NV - 8 * b), panel, 0.0)
        unit = jnp.where(lane < prow, panel, jnp.where(lane == prow, 1.0, 0.0))
        right = pltpu.roll(jnp.where(lane < 8, unit, panel) * inverse, NV - 8, 1)
        p0, p1, p2 = split(left)
        q0, q1, q2 = split(right)
        left = jnp.concatenate([p0, p0, p1, p0, p1, p2], axis=0).astype(BF16).T
        right = jnp.concatenate([q0, q1, q0, q2, q1, q0], axis=0).astype(BF16)
        rest = pltpu.roll(jnp.where(outside, mat[...], 0.0), NV - 8, 1) - dot_nn(left, right)
        mat[0 : NV - 8, :] = rest[8:, :]
        mat[NV - 8 :, :] = pltpu.roll(panel, NV - 8, 1)
        return carry

    lax.fori_loop(0, 7, eliminate, 0)
    gather(3, h_x, h_out)
    for side in range(2):
        @pl.when(sends("gx", side))
        def _():
            x_late(side, 1).start()
    lax.fori_loop(7, 16, eliminate, 0)

    row_of, lane_of = iota((NV, NV), 0), iota((NV, NV), 1)
    one = jnp.where(row_of == lane_of, 1.0, 0.0)
    done = mat[...]
    diag = jnp.sum(done * one, axis=1, keepdims=True)
    lower = jnp.where(row_of > lane_of, done, one) * lax.rsqrt(diag)
    linv[...] = lower
    linvt[...] = lower.T

    for i in range(len(LATE)):
        for side in range(2):
            @pl.when(receives("gx", side))
            def _():
                x_late(side, i).wait_recv()
    widen(True)

    lower = linv[...]
    hamil = gathered(3, h_out) * (-1.0 / (24.0 * ncell))
    raw = exact_nt(exact(lower, hamil), lower)
    shifted = 0.5 * (raw + raw.T) - one * (jnp.sum(raw * one) / NV)
    scale = lax.rsqrt(jnp.full((1, 1), jnp.sum(shifted * shifted) + 1e-06, F32))
    square = three(shifted, shifted) * (scale * scale)
    sign = shifted * scale
    for step in range(FILTER_STEPS):
        if step > 0:
            square = three(sign, sign)
        sign = 1.5 * sign - 0.5 * three(square, sign)
    rot = exact(linvt[...], exact(0.5 * (one - sign), lower))
    rot = (0.5 * (rot + rot.T)).astype(BF16)

    def densities(i, carry):
        for j in range(STACK):
            y = i * STACK + j
            own = ut[y + 2]
            mixed = dot_nn(rot, own)
            rows_d[pl.ds(y, 1), :] = jnp.sum(own.astype(F32) * mixed, axis=0, keepdims=True)
            rows_e[pl.ds(y, 1), :] = jnp.sum(appl[y] * mixed, axis=0, keepdims=True)
        return carry

    lax.fori_loop(0, CY // STACK, densities, 0)

    for side in range(2):
        @pl.when(sends("gx", side))
        def _():
            x_copy(side, 0, CY, 0).wait_send()

        @pl.when(sends("gy", side))
        def _():
            y_copy(side).wait_send()

        @pl.when(sends("gz", side))
        def _():
            whole = zs.at[:, side]
            pltpu.make_async_copy(whole, whole, z_send.at[side]).wait()


def to_cells(rows_d, rows_e, density, energy):
    density[...] = (rows_d[...].T * (1.0 / NB)).reshape(CX, CZ, CY)
    energy[...] = (rows_e[...].T * (-1.0 / (24.0 * NB))).reshape(CX, CZ, CY)


def body(subspace, potential):
    sizes = tuple(lax.axis_size(name) for name in AXES)
    nx, ny, nz = sizes
    vm, dma = pltpu.VMEM, pltpu.SemaphoreType.DMA
    any_space = pl.BlockSpec(memory_space=pltpu.HBM)
    whole = pl.BlockSpec(memory_space=pltpu.VMEM)
    rows_out = jax.ShapeDtypeStruct((CY, CELLS), F32)
    out = jax.ShapeDtypeStruct((CX, CZ, CY), F32)
    slices = ny * nz
    thin = NV // slices
    reduce_set = [
        vm((NV, NV), F32),
        vm((slices, thin, NV), F32), vm((slices, thin, NV), F32),
        vm((nx, thin, NV), F32), vm((slices, thin, NV), F32),
    ]
    rows_d, rows_e = pl.pallas_call(
        functools.partial(kernel, sizes),
        out_shape=(rows_out, rows_out),
        in_specs=[any_space, any_space],
        out_specs=(whole, whole),
        scratch_shapes=[
            vm((CX, CY, CZ, NV), BF16),
            vm((CY + 4, NV, CELLS), BF16),
            vm((CY, NV, CELLS), F32),
            vm((CY, NV, CELLS), BF16),
            vm((2, 2, CY, CZ, NV), BF16),
            vm((2, CX, 2, CZ, NV), BF16),
            vm((CY, 2, 2 * CX, NV), BF16),
            vm((CY, 2, 2 * CX, NV), BF16),
            vm((HALF, NV, NV), BF16),
            vm((CX, CZ, CY), F32),
            vm((CY, CELLS), F32),
            vm((CELLS, CELLS), BF16),
            vm((4 * CX, CELLS), BF16),
            vm((NV, CELLS), BF16),
            vm((CELLS, NV), BF16),
            vm((4 * CX, CELLS), BF16),
            *reduce_set,
            *reduce_set,
            vm((NV, NV), F32),
            vm((NV, NV), F32),
            vm((NV, NV), F32),
            dma((LOADS + 1,)),
            dma((2,)),
            dma((2, PIECES + len(LATE))),
            dma((2,)),
            dma((2,)),
            dma((2,)),
            dma((2, ZPIECES)),
            dma((2,)),
            dma((6,)),
        ],
        compiler_params=pltpu.CompilerParams(
            collective_id=0, has_side_effects=True, vmem_limit_bytes=55072 * 1024
        ),
    )(subspace, jnp.transpose(potential, (0, 2, 1)))
    density, energy = pl.pallas_call(
        to_cells,
        out_shape=(out, out),
        in_specs=[whole, whole],
        out_specs=(whole, whole),
        compiler_params=pltpu.CompilerParams(vmem_limit_bytes=8 * 1024 * 1024),
    )(rows_d, rows_e)
    return jnp.transpose(density, (0, 2, 1)), jnp.transpose(energy, (0, 2, 1))


def solution(mesh):
    return jax.shard_map(
        body,
        mesh=mesh,
        in_specs=(P("gx", "gy", "gz", None), P("gx", "gy", "gz")),
        out_specs=(P("gx", "gy", "gz"), P("gx", "gy", "gz")),
        check_vma=False,
    )
```
